512 devices in a mesh: space: 128 (over z, y, core), pair: 4 (over x).
Axes of the slice: x: 4, y: 8, z: 8, core: 2. Of those that a mesh axis runs over, the one named last changes fastest.
Arguments:
- positions: float32 [3, 262144], P(None, 'space'), may hold values from -1 to 1296, as said below
- polarizability: float32 [262144], P('space'), may hold values from 0.4 to 1.6
- charges: float32 [262144], P('space'), may hold values from -4 to 4
- groups: int32 [262144], P('space'), may hold values from 0 to 87380, never falling along the last dimension, each value on 1 to 6 neighbouring positions
- pair_list: int32 [128, 64, 2], P('space'), may hold values from 0 to 1023, as said below
- tile_count: int32 [128], P('space'), may hold values from 8 to 64, as said below
Outputs:
- dipoles: float32 [3, 262144], P(None, ('space', 'pair'))
- residual: float32 [3, 262144], P(None, ('space', 'pair'))
The draws below stay inside these ranges and needn't reach their ends.
Inputs may be any that keep to these rules, and one draw needn't show every extreme that they name: `positions`: Positions: block c sits on a lattice of spacing 2.15 in the cell of its row and column, with small displacements of each atom; no two atoms are closer than 1.2. `pair_list`: for entries t < tile_count[o]: column 0 is a slot 0 to 7 of row o; the partner's row is o, o + 1 or o + 2, and its column differs from the slot by at most one, counted around 8; with partner row o it is the slot itself or the next column. Each slot lists itself, and no pair twice. Entries at and after the count are padding. `tile_count`: number of listed entries of each row; some row lists all 64 candidate tiles.
All inputs are finite; a program needn't handle non-finite values.
Results may differ from the reference program's by a relative error of at most 0.00055.
Values sent between devices are 32-bit elements; how exact they have to be, the bound alone decides.
A program may use at most 64 MiB of HBM per device.

```python
import math
from functools import partial
import jax
import jax.numpy as jnp
import numpy as np
from jax import lax

BLK = 256
BPD = 8
ITERS = 3
OWNERS = 128
NBLK = 1024
NATOMS = 262144
TMAX = 64


def tile_plan(key):
    rows_all = NBLK // BPD
    row_list = jnp.arange(rows_all, dtype=jnp.int32)
    levels = jax.random.randint(jax.random.fold_in(key, 1), (rows_all,), 1, 7)
    busiest = jax.random.randint(jax.random.fold_in(key, 3), (), 0, rows_all - 2)
    levels = jnp.where(row_list == busiest, 8, levels)
    levels = jnp.where(row_list == rows_all - 1, 0, levels).astype(jnp.int32)
    coins = jax.random.randint(jax.random.fold_in(key, 2), (rows_all, BPD, 8), 0, 8)
    row_step = jnp.array([0, 0, 1, 1, 1, 2, 2, 2], jnp.int32)
    col_step = jnp.array([0, 1, -1, 0, 1, -1, 0, 1], jnp.int32)
    row_index = row_list[:, None, None]
    slot_index = jnp.arange(BPD, dtype=jnp.int32)[None, :, None]
    inside = row_index + row_step[None, None, :] < rows_all
    itself = ((row_step == 0) & (col_step == 0))[None, None, :]
    chosen = ((coins < levels[:, None, None]) | itself) & inside
    partner = (row_index + row_step[None, None, :]) * BPD + (slot_index + col_step[None, None, :] + BPD) % BPD
    slots_all = jnp.broadcast_to(slot_index, chosen.shape)
    chosen_flat = chosen.reshape(rows_all, TMAX)
    partner_flat = partner.reshape(rows_all, TMAX)
    slots_flat = slots_all.reshape(rows_all, TMAX)
    tile_index = jnp.arange(TMAX, dtype=jnp.int32)[None, :]
    scores = jnp.where(chosen_flat, tile_index, tile_index + TMAX)
    ordering = jnp.argsort(scores, axis=1)
    kept = jnp.take_along_axis(chosen_flat, ordering, 1)
    slot_sorted = jnp.where(kept, jnp.take_along_axis(slots_flat, ordering, 1), 0)
    padding = row_list[:, None] * BPD
    partner_sorted = jnp.where(kept, jnp.take_along_axis(partner_flat, ordering, 1), padding)
    pairs = jnp.stack([slot_sorted, partner_sorted], -1).astype(jnp.int32)
    counts = jnp.sum(chosen_flat.astype(jnp.int32), 1).astype(jnp.int32)
    return (pairs, counts)


def draw_pair_list(key, part):
    plan = tile_plan(key)
    return plan[0]


def draw_tile_count(key, part):
    plan = tile_plan(key)
    return plan[1]


def draw_positions(key, part):
    key = jax.random.fold_in(key, 11)
    atom_index = jnp.arange(NATOMS, dtype=jnp.int32)
    block_index = atom_index // BLK
    local_index = atom_index % BLK
    lattice_y = BLK // 32
    cell_x = local_index // (lattice_y * 4)
    cell_y = local_index // 4 % lattice_y
    cell_z = local_index % 4
    column = block_index % BPD
    row_number = block_index // BPD
    coord_x = (column * 8 + cell_x).astype(jnp.float32) * 2.15
    coord_y = cell_y.astype(jnp.float32) * 2.15
    coord_z = (row_number * 4 + cell_z).astype(jnp.float32) * 2.15
    lattice = jnp.stack([coord_x, coord_y, coord_z], 0)
    jitter = jnp.clip(0.15 * jax.random.normal(key, (3, NATOMS), jnp.float32), -0.45, 0.45)
    return (lattice + jitter).astype(jnp.float32)


def steps_of(key, extent, pieces, smallest, largest):
    loudness, own = 1.0, jax.random.fold_in(key, 6)
    for dim, shards_of in pieces:
        steps = jnp.exp(jax.random.uniform(jax.random.fold_in(own, dim), (shards_of,), jnp.float32, smallest / len(pieces), largest / len(pieces)))
        loudness = loudness * jnp.repeat(steps, extent[dim] // shards_of).reshape([-1 if axis == dim else 1 for axis in range(len(extent))])
    return loudness


def profile(amount, total, limit, slope):
    weights = [(1 << 20) // math.isqrt(standing ** slope) + 1 for standing in range(2, amount + 1)]
    spare, given = total - limit - (amount - 1), [1] * (amount - 1)
    while spare > 0:
        candidates = [i for i in range(amount - 1) if given[i] < limit]
        pool, remaining = sum([weights[i] for i in candidates]), spare
        for i in candidates:
            more = min(limit - given[i], max(1, remaining * weights[i] // pool), spare)
            given[i] = given[i] + more
            spare = spare - more
    return np.array([limit] + given)


def ragged_sizes(stream_key, amount, total, reach, slope):
    if amount == 2:
        one = jax.random.randint(stream_key, (), max(1, total - reach), min(reach, total - 1) + 1)
        return jnp.stack([one, total - one])
    tallies = jnp.asarray(profile(amount, total, reach, slope), jnp.int32)
    pairs = (amount - 1) // 2
    giver, receiver = tallies[1:1 + 2 * pairs:2], tallies[2:2 + 2 * pairs:2]
    room = jnp.minimum(giver - 1, reach - receiver)
    shifted = jax.random.randint(jax.random.fold_in(stream_key, 1), (pairs,), 0, 1 << 20) % (room + 1)
    tallies = tallies.at[1:1 + 2 * pairs:2].set(giver - shifted).at[2:2 + 2 * pairs:2].set(receiver + shifted)
    return tallies[jax.random.permutation(jax.random.fold_in(stream_key, 2), amount)]


def bell_draw(rng, extent, deviation, bound, cuts=(), kind=jnp.bfloat16):
    result = jax.random.normal(rng, extent, jnp.float32) * deviation
    if len(cuts) > 0:
        result = steps_of(rng, extent, cuts, -0.22, 0.18) * result
    return jnp.clip(result, min=-bound, max=bound).astype(kind)


def setup_inputs(seed: int = 0) -> dict:
    arg_keys = jax.random.split(jax.random.key(seed), 7)
    return {
        "positions": draw_positions(jax.random.fold_in(arg_keys[6], 71), 0),
        "polarizability": jnp.clip(jnp.exp(math.log(1.6) - 1.3862944 * jax.random.uniform(arg_keys[1], (NATOMS,), jnp.float32) ** steps_of(arg_keys[1], (NATOMS,), ((0, 128),), -0.2, 0.2)), 0.4, 1.6),
        "charges": bell_draw(arg_keys[2], (NATOMS,), 1.0, 4.0, ((0, 128),), jnp.float32),
        "groups": jnp.searchsorted(jnp.cumsum(ragged_sizes(arg_keys[3], NATOMS // 3, NATOMS, 6, 0)), jnp.arange(NATOMS), side="right").astype(jnp.int32),
        "pair_list": draw_pair_list(jax.random.fold_in(arg_keys[6], 71), 0),
        "tile_count": draw_tile_count(jax.random.fold_in(arg_keys[6], 71), 0),
    }


spacing = 2.15
thole_a = 0.39

def column_wrap(own_column, far_column):
    column_diff = far_column - own_column
    return (column_diff < -1).astype(jnp.int32) - (column_diff > 1).astype(jnp.int32)

def tile_terms(pos_i, pos_j, alpha_i, alpha_j, image_shift, self_tile):
    period = BPD * 8 * spacing
    offset = jnp.array([1.0, 0.0, 0.0], jnp.float32)[:, None] * (image_shift.astype(jnp.float32) * period)
    displacement = pos_i[:, :, None] - (pos_j + offset)[:, None, :]
    squared = lax.optimization_barrier(jnp.sum(displacement * displacement, 0))
    excluded = jnp.eye(pos_i.shape[1], dtype=jnp.float32) * self_tile
    padded_sq = squared + excluded
    inverse = lax.rsqrt(padded_sq)
    distance = padded_sq * inverse
    damp_radius = (alpha_i[:, None] * alpha_j[None, :]) ** (1.0 / 6.0)
    scaled = distance / damp_radius
    damping = thole_a * scaled * scaled * scaled
    decayed = jnp.exp(-damping)
    third_order = -jnp.expm1(-damping)
    fifth_order = third_order - damping * decayed
    retained = 1.0 - excluded
    inverse_cube = inverse * inverse * inverse
    coef_three = retained * third_order * inverse_cube
    coef_five = retained * 3.0 * fifth_order * inverse_cube * inverse * inverse
    return (displacement, coef_three, coef_five)

def charge_pair(displacement, coef_three, charge_i, charge_j, group_mask):
    weighted = coef_three * group_mask
    near_field = lax.optimization_barrier(jnp.sum(displacement * (weighted * charge_j[None, :])[None], 2))
    far_field = -lax.optimization_barrier(jnp.sum(displacement * (weighted * charge_i[:, None])[None], 1))
    return (near_field, far_field)

def dipole_pair(displacement, coef_three, coef_five, dipole_i, dipole_j):
    along_j = lax.optimization_barrier(jnp.sum(displacement * dipole_j[:, None, :], 0))
    near_field = lax.optimization_barrier(jnp.sum((coef_five * along_j)[None] * displacement, 2)) - lax.optimization_barrier(jnp.sum(coef_three[None] * dipole_j[:, None, :], 2))
    along_i = lax.optimization_barrier(jnp.sum(displacement * dipole_i[:, :, None], 0))
    far_field = lax.optimization_barrier(jnp.sum((coef_five * along_i)[None] * displacement, 1)) - lax.optimization_barrier(jnp.sum(coef_three[None] * dipole_i[:, :, None], 1))
    return (near_field, far_field)

def reference(positions, polarizability, charges, groups, pair_list, tile_count):
    block_pos = positions.reshape(3, NBLK, BLK).transpose(1, 0, 2)
    block_alpha = polarizability.reshape(NBLK, BLK)
    block_charge = charges.reshape(NBLK, BLK)
    block_group = groups.reshape(NBLK, BLK)

    def fields(block_vals, charged):

        def visit(owner_index, tile_row, total):
            own_slot = pair_list[owner_index, tile_row, 0]
            partner = pair_list[owner_index, tile_row, 1]
            own_block = owner_index * BPD + own_slot
            self_tile = (own_block == partner).astype(jnp.float32)
            image_shift = column_wrap(own_slot, partner % BPD)
            displacement, coef_three, coef_five = tile_terms(block_pos[own_block], block_pos[partner], block_alpha[own_block], block_alpha[partner], image_shift, self_tile)
            if charged:
                group_mask = (block_group[own_block][:, None] != block_group[partner][None, :]).astype(jnp.float32)
                near_field, far_field = charge_pair(displacement, coef_three, block_charge[own_block], block_charge[partner], group_mask)
            else:
                near_field, far_field = dipole_pair(displacement, coef_three, coef_five, block_vals[own_block], block_vals[partner])
            total = total.at[own_block].add(near_field)
            return total.at[partner].add(far_field * (1.0 - self_tile))

        def owner_pass(owner_index, total):
            return lax.fori_loop(0, tile_count[owner_index], partial(visit, owner_index), total)
        total = lax.fori_loop(0, OWNERS, owner_pass, jnp.zeros((NBLK, 3, BLK), jnp.float32))
        return total.transpose(1, 0, 2).reshape(3, NATOMS)

    def mutual(vectors):
        return fields(vectors.reshape(3, NBLK, BLK).transpose(1, 0, 2), False)
    alpha_row = polarizability[None, :]
    direct_field = fields(None, True)
    dipoles = alpha_row * direct_field
    residual = mutual(dipoles)
    precond = alpha_row * residual
    direction = precond
    rz_value = jnp.sum(residual * precond)
    for iteration in range(ITERS):
        image_vec = direction / alpha_row - mutual(direction)
        length = rz_value / jnp.sum(direction * image_vec)
        dipoles = dipoles + length * direction
        residual = residual - length * image_vec
        precond = alpha_row * residual
        rz_next = jnp.sum(residual * precond)
        direction = precond + rz_next / rz_value * direction
        rz_value = rz_next
    return (dipoles, residual)
```

```python
import functools

import jax
import jax.numpy as jnp
from jax import lax
from jax.experimental import pallas as pl
from jax.experimental.pallas import tpu as pltpu
from jax.sharding import PartitionSpec as P

BLK = 256
BPD = 8
ITERS = 3
LANES = 128
ROWS = 32
GROUPS = BLK // ROWS
PERIOD = BPD * 8 * 2.15
THOLE = 0.39
SWEEPS = ITERS + 1
MESH = pl.DeviceIdType.MESH

HALO = [(d, e) for d in (-2, -1, 0, 1, 2) for e in (-1, 0, 1) if (d, e) != (0, 0)]
AHEAD = [-2, -1, 1, 2]
GRAM = [(i, j) for i in range(ITERS) for j in range(i, ITERS + 1)]


def kernel(
    spaces,
    pairs,
    span_y,
    attr_ref,
    dip_ref,
    res_ref,
    window,
    column,
    weight,
    coef,
    acc,
    alpha,
    direct,
    vec,
    field,
    gram,
    send_sem,
    recv_sem,
):
    sp = lax.axis_index("space")
    pr = lax.axis_index("pair")
    core = lax.rem(sp, 2)
    y = lax.rem(sp // 2, span_y)
    z = sp // (2 * span_y)
    span_z = spaces // (2 * span_y)

    def at_space(d):
        return lax.rem(sp + (d + spaces), spaces)

    def at_pair(e):
        return lax.rem(pr + (e + pairs), pairs)

    def at_core(c):
        return sp - core + lax.rem(core + c, 2)

    stages = [
        (
            [(at_core(c), at_pair(k)) for k in range(pairs) for c in range(2) if (k, c) != (0, 0)],
            pr * 2 + core,
        ),
        (
            [(sp + (lax.rem(y + k, span_y) - y) * 2, pr) for k in range(1, span_y)],
            y,
        ),
        (
            [(sp + (lax.rem(z + k, span_z) - z) * 2 * span_y, pr) for k in range(1, span_z)],
            z,
        ),
    ]

    barrier = pltpu.get_barrier_semaphore()
    partners = [(at_space(d), at_pair(e)) for d, e in HALO]
    for members, _ in stages:
        partners = partners + members
    for partner in partners:
        pl.semaphore_signal(barrier, inc=1, device_id=partner, device_id_type=MESH)

    for k in range(4):
        block = lax.rem(2 * pr + (k - 1 + BPD), BPD)
        window[2, :, k * BLK : (k + 1) * BLK] = attr_ref[
            :, pl.ds(pl.multiple_of(block * BLK, BLK), BLK)
        ]
    low = jnp.where(pr == 0, -PERIOD, 0.0).astype(jnp.float32)
    high = jnp.where(pr == pairs - 1, PERIOD, 0.0).astype(jnp.float32)
    window[2, 0:1, 0:BLK] = window[2, 0:1, 0:BLK] + low
    window[2, 0:1, 3 * BLK :] = window[2, 0:1, 3 * BLK :] + high

    for a in range(2):
        for c in range(2):
            lanes = pl.ds((a + 1) * BLK + c * LANES, LANES)
            turned = window[2, 0:8, lanes].T
            for k, row in enumerate((0, 1, 2, 5, 6)):
                values = jnp.broadcast_to(turned[:, row : row + 1], (LANES, LANES))
                if row == 6:
                    values = values * THOLE
                column[a, k, c * LANES : (c + 1) * LANES, :] = values
            share = window[2, 3:4, lanes]
            for k in range(3):
                alpha[a, 2 * k + c : 2 * k + c + 1, :] = share
        alpha[a, 6:8, :] = jnp.zeros((2, LANES), jnp.float32)

    pl.semaphore_wait(barrier, len(partners))

    def attr_copy(index, d):
        return pltpu.make_async_remote_copy(
            src_ref=window.at[2],
            dst_ref=window.at[2 - d],
            send_sem=send_sem.at[index],
            recv_sem=recv_sem.at[index],
            device_id=(at_space(d), pr),
            device_id_type=MESH,
        )

    for index, d in enumerate(AHEAD):
        attr_copy(index, d).start()

    def weigh(a, row, step):
        slot = a * 15 + row * 3 + step
        dx = step - 1
        own, far = (a + 1) * BLK, (a + step) * BLK
        if row == 2:
            entry, lane = (8 + abs(dx), far if dx < 0 else own)
        elif row > 2:
            entry, lane = (8 + (2, 5)[row - 3] + dx + 1, own)
        else:
            entry, lane = (8 + (5, 2)[row] - dx + 1, far)
        source = 2 if row >= 2 else row
        weight[slot : slot + 1, :] = window[source, entry : entry + 1, lane : lane + LANES]

    def build(a, rows, row, step, c, totals, itself):
        lanes = pl.ds(pl.multiple_of((a + step) * BLK + c * LANES, LANES), LANES)

        def far(entry):
            return window[row, entry : entry + 1, lanes]

        rx = column[a, 0, rows, :] - far(0)
        ry = column[a, 1, rows, :] - far(1)
        rz = column[a, 2, rows, :] - far(2)
        squared = jnp.maximum(rx * rx + ry * ry + rz * rz, 1.0)
        inverse = lax.rsqrt(squared)
        inverse_sq = inverse * inverse
        damping = (squared * (squared * inverse)) * (column[a, 4, rows, :] * far(6))
        decayed = jnp.exp(-damping)
        third = 1.0 - decayed
        fifth = third - damping * decayed
        tile = a * 15 + row * 3 + step
        weighted = (inverse_sq * inverse) * weight[pl.ds(tile, 1), :]
        three = third * weighted
        five = (fifth * inverse_sq) * (weighted * 3.0)
        root = five * lax.rsqrt(jnp.maximum(five, 1e-30))
        index = tile * 2 + c
        coef[index, 0, rows, :] = rx * root
        coef[index, 1, rows, :] = ry * root
        coef[index, 2, rows, :] = rz * root
        if itself:
            shape = (ROWS, LANES)
            own = lax.broadcasted_iota(jnp.int32, shape, 0) + rows.start
            other = lax.broadcasted_iota(jnp.int32, shape, 1) + c * LANES
            coef[index, 3, rows, :] = jnp.where(own == other, 0.0, three)
        else:
            coef[index, 3, rows, :] = three
        charged = jnp.where(column[a, 3, rows, :] != far(5), three * far(4), 0.0)
        ex, ey, ez = totals
        return (ex + charged * rx, ey + charged * ry, ez + charged * rz)

    def apply(n, a, rows, row, step, c, totals):
        index = (a * 15 + row * 3 + step) * 2 + c
        sx, sy, sz, three = (coef[index, k, rows, :] for k in range(4))
        vx, vy, vz = (vec[n, row, a + step, 2 * k + c : 2 * k + c + 1, :] for k in range(3))
        along = sx * vx + sy * vy + sz * vz
        ex, ey, ez = totals
        return (
            ex + (along * sx - three * vx),
            ey + (along * sy - three * vy),
            ez + (along * sz - three * vz),
        )

    def zeros():
        return tuple(jnp.zeros((ROWS, LANES), jnp.float32) for _ in range(3))

    def place(group):
        a = group // GROUPS
        return a, pl.ds(pl.multiple_of((group - a * GROUPS) * ROWS, ROWS), ROWS)

    def load_acc(a, rows):
        return tuple(acc[a, k, rows, :] for k in range(3))

    def store_acc(a, rows, totals):
        for k in range(3):
            acc[a, k, rows, :] = totals[k]

    def summed(a):
        parts = []
        for k in range(3):
            for c in range(2):
                turned = acc[a, k, c * LANES : (c + 1) * LANES, :].T
                parts.append(jnp.sum(turned, axis=0, keepdims=True))
        parts.append(jnp.zeros((2, LANES), jnp.float32))
        return jnp.concatenate(parts, axis=0)

    for a in range(2):
        for step in range(3):
            for row in (2, 3, 4):
                weigh(a, row, step)

    def build_own(group, carry):
        a, rows = place(group)
        totals = zeros()
        for step in range(3):
            for c in range(2):
                totals = build(a, rows, 2, step, c, totals, step == 1)
        store_acc(a, rows, totals)
        return carry

    lax.fori_loop(0, 2 * GROUPS, build_own, 0)
    for index, d in enumerate(AHEAD):
        attr_copy(index, d).wait()
    for a in range(2):
        for step in range(3):
            for row in (0, 1):
                weigh(a, row, step)

    def build_rest(group, carry):
        a, rows = place(group)

        def one_row(index, totals):
            row = index + index // 2
            for step in range(3):
                for c in range(2):
                    totals = build(a, rows, row, step, c, totals, False)
            return totals

        store_acc(a, rows, lax.fori_loop(0, 4, one_row, load_acc(a, rows)))
        return carry

    lax.fori_loop(0, 2 * GROUPS, build_rest, 0)
    for a in range(2):
        value = summed(a)
        direct[a] = value
        vec[0, 2, a + 1] = value * alpha[a]

    base = len(AHEAD)

    def halo_copy(n, index):
        d, e = HALO[index]
        if e == 0:
            source = vec.at[n, 2, pl.ds(1, 2)]
            target = vec.at[n, 2 - d, pl.ds(1, 2)]
        elif e == 1:
            source = vec.at[n, 2, pl.ds(2, 1)]
            target = vec.at[n, 2 - d, pl.ds(0, 1)]
        else:
            source = vec.at[n, 2, pl.ds(1, 1)]
            target = vec.at[n, 2 - d, pl.ds(3, 1)]
        place_of = base + n * len(HALO) + index
        return pltpu.make_async_remote_copy(
            src_ref=source,
            dst_ref=target,
            send_sem=send_sem.at[place_of],
            recv_sem=recv_sem.at[place_of],
            device_id=(at_space(d), at_pair(e)),
            device_id_type=MESH,
        )

    def sweep(n, carry):
        for index in range(len(HALO)):
            halo_copy(n, index).start()

        def near(group, inner):
            a, rows = place(group)
            totals = zeros()
            for far in range(2):
                for c in range(2):
                    totals = apply(n, a, rows, 2, far + 1 - a, c, totals)
            store_acc(a, rows, totals)
            return inner

        lax.fori_loop(0, 2 * GROUPS, near, 0)
        for index in range(len(HALO)):
            halo_copy(n, index).wait()

        def rest(group, inner):
            a, rows = place(group)
            totals = load_acc(a, rows)
            for c in range(2):
                totals = apply(n, a, rows, 2, 2 * a, c, totals)

            def one_row(index, totals):
                row = index + index // 2
                for step in range(3):
                    for c in range(2):
                        totals = apply(n, a, rows, row, step, c, totals)
                return totals

            store_acc(a, rows, lax.fori_loop(0, 4, one_row, totals))
            return inner

        lax.fori_loop(0, 2 * GROUPS, rest, 0)
        for a in range(2):
            value = summed(a)
            field[n, a] = value
            vec[n + 1, 2, a + 1] = value * alpha[a]
        return carry

    lax.fori_loop(0, SWEEPS, sweep, 0)

    lines = []
    for i, j in GRAM:
        product = field[i, 0] * (alpha[0] * field[j, 0]) + field[i, 1] * (alpha[1] * field[j, 1])
        lines.append(jnp.sum(product, axis=0, keepdims=True))
    lines.append(jnp.zeros((16 - len(GRAM), LANES), jnp.float32))
    total = jnp.concatenate(lines, axis=0)
    first = base + SWEEPS * len(HALO)
    for stage, (members, mine) in enumerate(stages):
        gram[stage, mine] = total
        copies = []
        for index, member in enumerate(members):
            copies.append(
                pltpu.make_async_remote_copy(
                    src_ref=gram.at[stage, mine],
                    dst_ref=gram.at[stage, mine],
                    send_sem=send_sem.at[first + index],
                    recv_sem=recv_sem.at[first + index],
                    device_id=member,
                    device_id_type=MESH,
                )
            )
            copies[-1].start()
        for copy in copies:
            copy.wait()
        first += len(members)
        total = gram[stage, 0]
        for index in range(1, len(members) + 1):
            total = total + gram[stage, index]

    sums = jnp.broadcast_to(jnp.sum(total, axis=1, keepdims=True), (16, LANES))
    entry = {}
    for index, (i, j) in enumerate(GRAM):
        entry[i, j] = entry[j, i] = sums[index : index + 1, :]

    def inner(left, right):
        value = None
        for i, u in enumerate(left):
            for j, v in enumerate(right):
                term = u * v * entry[i, j]
                value = term if value is None else value + term
        return value

    one = jnp.ones((1, LANES), jnp.float32)
    residual, direction = [one], [one]
    dipole = []
    rz_value = inner(residual, residual)
    for iteration in range(ITERS):
        size = iteration + 1
        image = [
            (direction[k] if k < size else 0.0) - (direction[k - 1] if k > 0 else 0.0)
            for k in range(size + 1)
        ]
        length = rz_value / inner(direction, image)
        dipole = [
            length * direction[k] + (dipole[k] if k < len(dipole) else 0.0) for k in range(size)
        ]
        residual = [
            (residual[k] if k < size else 0.0) - length * image[k] for k in range(size + 1)
        ]
        if iteration + 1 < ITERS:
            rz_next = inner(residual, residual)
            ratio = rz_next / rz_value
            direction = [
                residual[k] + (ratio * direction[k] if k < size else 0.0) for k in range(size + 1)
            ]
            rz_value = rz_next

    for a in range(2):
        moved = direct[a]
        for k in range(ITERS):
            moved = moved + dipole[k] * field[k, a]
        moved = moved * alpha[a]
        left = residual[0] * field[0, a]
        for k in range(1, ITERS + 1):
            left = left + residual[k] * field[k, a]
        for k in range(3):
            for c in range(2):
                lanes = slice(a * BLK + c * LANES, a * BLK + (c + 1) * LANES)
                dip_ref[k : k + 1, lanes] = moved[2 * k + c : 2 * k + c + 1, :]
                res_ref[k : k + 1, lanes] = left[2 * k + c : 2 * k + c + 1, :]


def on_device(spaces, pairs, span_y, positions, polarizability, charges, groups, pair_list, tile_count):
    atoms = positions.shape[1]
    row = lax.axis_index("space")
    slot, partner = pair_list[0, :, 0], pair_list[0, :, 1]
    row_step = partner // BPD - row
    col_step = (partner % BPD - slot + (BPD + 1)) % BPD - 1
    kind = jnp.where(row_step == 0, col_step, row_step * 3 + col_step)
    listed = jnp.arange(pair_list.shape[1]) < tile_count[0]
    key = jnp.where(listed, kind * BPD + slot, -1)
    wanted = jnp.arange(8 * BPD)
    flags = jnp.max((key[:, None] == wanted[None, :]).astype(jnp.float32), axis=0)
    flags = jnp.broadcast_to(flags.reshape(8, BPD, 1), (8, BPD, BLK)).reshape(8, atoms)
    attrs = jnp.concatenate(
        [
            positions,
            polarizability[None],
            charges[None],
            groups.astype(jnp.float32)[None],
            lax.rsqrt(polarizability)[None],
            jnp.zeros((1, atoms), jnp.float32),
            flags,
        ],
        0,
    )
    copies = len(AHEAD) + SWEEPS * len(HALO) + 2 * pairs + span_y + spaces // (2 * span_y) - 3
    share = jax.ShapeDtypeStruct((3, 2 * BLK), jnp.float32)
    vmem = pl.BlockSpec(memory_space=pltpu.VMEM)
    return pl.pallas_call(
        functools.partial(kernel, spaces, pairs, span_y),
        out_shape=(share, share),
        in_specs=[vmem],
        out_specs=(vmem, vmem),
        scratch_shapes=[
            pltpu.VMEM((5, 16, 4 * BLK), jnp.float32),
            pltpu.VMEM((2, 5, BLK, LANES), jnp.float32),
            pltpu.VMEM((32, LANES), jnp.float32),
            pltpu.VMEM((60, 4, BLK, LANES), jnp.float32),
            pltpu.VMEM((2, 3, BLK, LANES), jnp.float32),
            pltpu.VMEM((2, 8, LANES), jnp.float32),
            pltpu.VMEM((2, 8, LANES), jnp.float32),
            pltpu.VMEM((SWEEPS + 1, 5, 4, 8, LANES), jnp.float32),
            pltpu.VMEM((SWEEPS, 2, 8, LANES), jnp.float32),
            pltpu.VMEM((3, 8, 16, LANES), jnp.float32),
            pltpu.SemaphoreType.DMA((copies,)),
            pltpu.SemaphoreType.DMA((copies,)),
        ],
        compiler_params=pltpu.CompilerParams(
            collective_id=0, has_side_effects=True, vmem_limit_bytes=52 * 2**20
        ),
    )(attrs)


def solution(mesh):
    spaces, pairs = mesh.shape["space"], mesh.shape["pair"]
    span_y = 8 if spaces >= 128 else 2
    return jax.shard_map(
        functools.partial(on_device, spaces, pairs, span_y),
        mesh=mesh,
        in_specs=(
            P(None, "space"),
            P("space"),
            P("space"),
            P("space"),
            P("space", None, None),
            P("space"),
        ),
        out_specs=(P(None, ("space", "pair")), P(None, ("space", "pair"))),
        check_vma=False,
    )
```

```python
import functools

import jax
import jax.numpy as jnp
from jax import lax
from jax.experimental import pallas as pl
from jax.experimental.pallas import tpu as pltpu
from jax.sharding import PartitionSpec as P

BLK = 256
BPD = 8
ITERS = 3
LANES = 128
SUBS = 8
TILES = BLK // SUBS
BUILD = 4
APPLY = 8
PERIOD = BPD * 8 * 2.15
THOLE = 0.39
SWEEPS = ITERS + 1
MESH = pl.DeviceIdType.MESH

NEAR = [-2, -1, 1, 2]
REACH = [-2, 2, -1, 1, 0]
TARGETS = {1: (0, 0, NEAR), 3: (0, -1, REACH), 2: (1, 0, NEAR), 0: (1, 1, REACH)}
HALO = [(column, d) for column in (1, 3, 2, 0) for d in TARGETS[column][2]]
X, Y, Z, GROUP, ROOT, CHARGE = range(6)
GRAM = [(i, j) for i in range(ITERS) for j in range(i, ITERS + 1)]


def kernel(
    spaces,
    pairs,
    span_y,
    positions_ref,
    polar_ref,
    charges_ref,
    groups_ref,
    list_ref,
    count_ref,
    dip_ref,
    res_ref,
    positions,
    polar,
    charges,
    groups,
    listing,
    flags,
    window,
    wide,
    column,
    weight,
    coef,
    acc,
    alpha,
    direct,
    vec,
    spread,
    field,
    gram,
    load_sem,
    send_sem,
    recv_sem,
):
    loads = [
        pltpu.make_async_copy(source, target, load_sem.at[index])
        for index, (source, target) in enumerate(
            (
                (positions_ref, positions),
                (polar_ref, polar),
                (charges_ref, charges),
                (groups_ref, groups),
                (list_ref, listing),
            )
        )
    ]
    for load in loads:
        load.start()

    sp = lax.axis_index("space")
    pr = lax.axis_index("pair")
    core = lax.rem(sp, 2)
    y = lax.rem(sp // 2, span_y)
    z = sp // (2 * span_y)
    span_z = spaces // (2 * span_y)

    def at_space(d):
        return lax.rem(sp + (d + spaces), spaces)

    def at_pair(e):
        return lax.rem(pr + (e + pairs), pairs)

    def at_core(c):
        return sp - core + lax.rem(core + c, 2)

    stages = [
        (
            [(at_core(c), at_pair(k)) for k in range(pairs) for c in range(2) if (k, c) != (0, 0)],
            pr * 2 + core,
        ),
        (
            [(sp + (lax.rem(y + k, span_y) - y) * 2, pr) for k in range(1, span_y)],
            y,
        ),
        (
            [(sp + (lax.rem(z + k, span_z) - z) * 2 * span_y, pr) for k in range(1, span_z)],
            z,
        ),
    ]

    barrier = pltpu.get_barrier_semaphore()
    partners = [(at_space(d), at_pair(e)) for d in REACH for e in (-1, 0, 1) if (d, e) != (0, 0)]
    for members, _ in stages:
        partners = partners + members
    for partner in partners:
        pl.semaphore_signal(barrier, inc=1, device_id=partner, device_id_type=MESH)

    for load in loads:
        load.wait()

    slot, partner = listing[0:1, :], listing[1:2, :]
    row_step = partner // BPD - sp
    col_step = (partner % BPD - slot + (BPD + 1)) % BPD - 1
    kind = jnp.where(row_step == 0, col_step, row_step * 3 + col_step)
    entry = lax.broadcasted_iota(jnp.int32, slot.shape, 1)
    key = jnp.where(entry < count_ref[0], kind * BPD + slot, -1)
    wanted = lax.broadcasted_iota(jnp.int32, (32, slot.shape[1]), 0)
    wanted = (wanted // 4) * BPD + (2 * pr + (BPD - 1) + wanted % 4) % BPD
    found = jnp.max((key == wanted).astype(jnp.float32), axis=1, keepdims=True)
    flags[...] = jnp.broadcast_to(found, (32, LANES))

    low = jnp.where(pr == 0, -PERIOD, 0.0).astype(jnp.float32)
    high = jnp.where(pr == pairs - 1, PERIOD, 0.0).astype(jnp.float32)
    for k in range(4):
        block = lax.rem(2 * pr + (k - 1 + BPD), BPD)
        for c in range(2):
            lanes = pl.ds(pl.multiple_of(block * BLK + c * LANES, LANES), LANES)
            shift = {0: low, 3: high}.get(k, 0.0)
            lines = {
                X: positions[0:1, lanes] + shift,
                Y: positions[1:2, lanes],
                Z: positions[2:3, lanes],
                GROUP: groups[0:1, lanes].astype(jnp.float32),
                ROOT: lax.rsqrt(polar[0:1, lanes]),
                CHARGE: charges[0:1, lanes],
            }
            for line, value in lines.items():
                window[2, k, c, line : line + 1, :] = value
            window[2, k, c, 6:8, :] = jnp.zeros((2, LANES), jnp.float32)
            if k in (1, 2):
                for m in range(3):
                    alpha[k - 1, 2 * m + c : 2 * m + c + 1, :] = polar[0:1, lanes]
        for m in range(8):
            window[2, k, 2, m : m + 1, :] = flags[4 * m + k : 4 * m + k + 1, :]

    for a in range(2):
        for c in range(2):
            turned = window[2, a + 1, c].T
            for k in (X, Y, Z, GROUP, ROOT):
                values = jnp.broadcast_to(turned[:, k : k + 1], (LANES, LANES))
                if k == ROOT:
                    values = values * THOLE
                half = LANES // SUBS
                column[a, k, c * half : (c + 1) * half] = values.reshape(half, SUBS, LANES)
        alpha[a, 6:8, :] = jnp.zeros((2, LANES), jnp.float32)

    def widen(row, col):
        for c in range(2):
            for k in range(6):
                line = window[row, col, c, k : k + 1, :]
                wide[row, col, c, k] = jnp.broadcast_to(line, (SUBS, LANES))

    def widen_own(col, carry):
        widen(2, col)
        return carry

    def widen_rest(index, carry):
        row = index // 4
        widen(row + row // 2, index % 4)
        return carry

    pl.semaphore_wait(barrier, len(partners))

    def attr_copy(index, d):
        return pltpu.make_async_remote_copy(
            src_ref=window.at[2],
            dst_ref=window.at[2 - d],
            send_sem=send_sem.at[index],
            recv_sem=recv_sem.at[index],
            device_id=(at_space(d), pr),
            device_id_type=MESH,
        )

    for index, d in enumerate(NEAR):
        attr_copy(index, d).start()

    def weigh(a, row, step):
        slot = a * 15 + row * 3 + step
        dx = step - 1
        if row == 2:
            entry, col = (abs(dx), a + step if dx < 0 else a + 1)
        elif row > 2:
            entry, col = ((2, 5)[row - 3] + dx + 1, a + 1)
        else:
            entry, col = ((5, 2)[row] - dx + 1, a + step)
        line = window[min(row, 2), col, 2, entry : entry + 1, :]
        weight[slot] = jnp.broadcast_to(line, (SUBS, LANES))

    def build(a, part, row, step, c, totals, itself):
        def far(line):
            return wide[row, a + step, c, line]

        rx = column[a, X, part] - far(X)
        ry = column[a, Y, part] - far(Y)
        rz = column[a, Z, part] - far(Z)
        squared = jnp.maximum(rx * rx + ry * ry + rz * rz, 1.0)
        inverse = lax.rsqrt(squared)
        inverse_sq = inverse * inverse
        damping = (squared * (squared * inverse)) * (column[a, ROOT, part] * far(ROOT))
        decayed = jnp.exp(-damping)
        third = 1.0 - decayed
        fifth = third - damping * decayed
        tile = a * 15 + row * 3 + step
        weighted = (inverse_sq * inverse) * weight[tile]
        three = third * weighted
        five = (fifth * inverse_sq) * (weighted * 3.0)
        root = five * lax.rsqrt(jnp.maximum(five, 1e-30))
        index = tile * 2 + c
        coef[index, 0, part] = rx * root
        coef[index, 1, part] = ry * root
        coef[index, 2, part] = rz * root
        if itself:
            shape = (BUILD, SUBS, LANES)
            own = lax.broadcasted_iota(jnp.int32, shape, 0) * SUBS + part.start * SUBS
            own = own + lax.broadcasted_iota(jnp.int32, shape, 1)
            other = lax.broadcasted_iota(jnp.int32, shape, 2) + c * LANES
            coef[index, 3, part] = jnp.where(own == other, 0.0, three)
        else:
            coef[index, 3, part] = three
        charged = jnp.where(column[a, GROUP, part] != far(GROUP), three * far(CHARGE), 0.0)
        ex, ey, ez = totals
        return (ex + charged * rx, ey + charged * ry, ez + charged * rz)

    def apply(a, part, row, step, c, totals):
        index = (a * 15 + row * 3 + step) * 2 + c
        sx, sy, sz, three = (coef[index, k, part] for k in range(4))
        vx, vy, vz = (spread[row, a + step, 2 * k + c] for k in range(3))
        along = sx * vx + sy * vy + sz * vz
        ex, ey, ez = totals
        return (
            ex + (along * sx - three * vx),
            ey + (along * sy - three * vy),
            ez + (along * sz - three * vz),
        )

    def zeros(size):
        return tuple(jnp.zeros((size, SUBS, LANES), jnp.float32) for _ in range(3))

    def load_acc(a, part):
        return tuple(acc[a, k, part] for k in range(3))

    def store_acc(a, part, totals):
        for k in range(3):
            acc[a, k, part] = totals[k]

    def summed(a):
        parts = []
        for k in range(3):
            for c in range(2):
                half = LANES // SUBS
                turned = acc[a, k, c * half : (c + 1) * half].reshape(LANES, LANES).T
                parts.append(jnp.sum(turned, axis=0, keepdims=True))
        parts.append(jnp.zeros((2, LANES), jnp.float32))
        return jnp.concatenate(parts, axis=0)

    base = len(NEAR)

    def halo_copy(n, index):
        col, d = HALO[index]
        block, e, _ = TARGETS[col]
        number = base + n * len(HALO) + index
        return pltpu.make_async_remote_copy(
            src_ref=vec.at[n, 2, block + 1],
            dst_ref=vec.at[n, 2 - d, col],
            send_sem=send_sem.at[number],
            recv_sem=recv_sem.at[number],
            device_id=(at_space(d), at_pair(e)),
            device_id_type=MESH,
        )

    def send(n, block):
        for index, (col, _) in enumerate(HALO):
            if TARGETS[col][0] == block:
                halo_copy(n, index).start()

    def arrive(n, wanted_col):
        for index, (col, _) in enumerate(HALO):
            if col == wanted_col:
                halo_copy(n, index).wait()

    for a in range(2):
        for step in range(3):
            for row in (2, 3, 4):
                weigh(a, row, step)

    lax.fori_loop(0, 4, widen_own, 0)

    def build_own(group, carry):
        a = group // (TILES // BUILD)
        part = pl.ds((group - a * (TILES // BUILD)) * BUILD, BUILD)
        totals = zeros(BUILD)
        for step in range(3):
            for c in range(2):
                totals = build(a, part, 2, step, c, totals, step == 1)
        store_acc(a, part, totals)
        return carry

    lax.fori_loop(0, 2 * (TILES // BUILD), build_own, 0)
    for index, d in enumerate(NEAR):
        attr_copy(index, d).wait()
    for a in range(2):
        for step in range(3):
            for row in (0, 1):
                weigh(a, row, step)
    lax.fori_loop(0, 16, widen_rest, 0)

    def build_rest(a, carry):
        def one_group(group, inner):
            part = pl.ds(group * BUILD, BUILD)

            def one_row(index, totals):
                row = index + index // 2
                for step in range(3):
                    for c in range(2):
                        totals = build(a, part, row, step, c, totals, False)
                return totals

            store_acc(a, part, lax.fori_loop(0, 4, one_row, load_acc(a, part)))
            return inner

        lax.fori_loop(0, TILES // BUILD, one_group, 0)
        value = summed(a)
        direct[a] = value
        vec[0, 2, a + 1] = value * alpha[a]
        for block in range(2):

            @pl.when(a == block)
            def _():
                send(0, block)

        return carry

    lax.fori_loop(0, 2, build_rest, 0)

    def ready(n, col):
        arrive(n, col)

        def one_row(row, carry):
            for m in range(6):
                line = vec[n, row, col, m : m + 1, :]
                spread[row, col, m] = jnp.broadcast_to(line, (SUBS, LANES))
            return carry

        lax.fori_loop(0, 5, one_row, 0)

    def strips(a, steps, fresh):
        def one_group(group, carry):
            part = pl.ds(group * APPLY, APPLY)
            totals = zeros(APPLY) if fresh else load_acc(a, part)
            for step in steps:
                for row in range(5):
                    for c in range(2):
                        totals = apply(a, part, row, step, c, totals)
            store_acc(a, part, totals)
            return carry

        lax.fori_loop(0, TILES // APPLY, one_group, 0)

    def finish(n, a):
        value = summed(a)
        field[n, a] = value
        vec[n + 1, 2, a + 1] = value * alpha[a]

        @pl.when(n + 1 < SWEEPS)
        def _():
            send(n + 1, a)

    def sweep(n, carry):
        ready(n, 1)
        strips(0, (1,), True)
        strips(1, (0,), True)
        ready(n, 2)
        ready(n, 0)
        strips(0, (0, 2), False)
        finish(n, 0)
        ready(n, 3)
        strips(1, (2, 1), False)
        finish(n, 1)
        return carry

    lax.fori_loop(0, SWEEPS, sweep, 0)

    lines = []
    for i, j in GRAM:
        product = field[i, 0] * (alpha[0] * field[j, 0]) + field[i, 1] * (alpha[1] * field[j, 1])
        lines.append(jnp.sum(product, axis=0, keepdims=True))
    lines.append(jnp.zeros((16 - len(GRAM), LANES), jnp.float32))
    total = jnp.concatenate(lines, axis=0)
    first = base + SWEEPS * len(HALO)
    for stage, (members, mine) in enumerate(stages):
        gram[stage, mine] = total
        copies = []
        for index, member in enumerate(members):
            copies.append(
                pltpu.make_async_remote_copy(
                    src_ref=gram.at[stage, mine],
                    dst_ref=gram.at[stage, mine],
                    send_sem=send_sem.at[first + index],
                    recv_sem=recv_sem.at[first + index],
                    device_id=member,
                    device_id_type=MESH,
                )
            )
            copies[-1].start()
        for copy in copies:
            copy.wait()
        first += len(members)
        total = gram[stage, 0]
        for index in range(1, len(members) + 1):
            total = total + gram[stage, index]

    sums = jnp.broadcast_to(jnp.sum(total, axis=1, keepdims=True), (16, LANES))
    entry = {}
    for index, (i, j) in enumerate(GRAM):
        entry[i, j] = entry[j, i] = sums[index : index + 1, :]

    def inner(left, right):
        value = None
        for i, u in enumerate(left):
            for j, v in enumerate(right):
                term = u * v * entry[i, j]
                value = term if value is None else value + term
        return value

    one = jnp.ones((1, LANES), jnp.float32)
    residual, direction = [one], [one]
    dipole = []
    rz_value = inner(residual, residual)
    for iteration in range(ITERS):
        size = iteration + 1
        image = [
            (direction[k] if k < size else 0.0) - (direction[k - 1] if k > 0 else 0.0)
            for k in range(size + 1)
        ]
        length = rz_value / inner(direction, image)
        dipole = [
            length * direction[k] + (dipole[k] if k < len(dipole) else 0.0) for k in range(size)
        ]
        residual = [
            (residual[k] if k < size else 0.0) - length * image[k] for k in range(size + 1)
        ]
        if iteration + 1 < ITERS:
            rz_next = inner(residual, residual)
            ratio = rz_next / rz_value
            direction = [
                residual[k] + (ratio * direction[k] if k < size else 0.0) for k in range(size + 1)
            ]
            rz_value = rz_next

    for a in range(2):
        moved = direct[a]
        for k in range(ITERS):
            moved = moved + dipole[k] * field[k, a]
        moved = moved * alpha[a]
        left = residual[0] * field[0, a]
        for k in range(1, ITERS + 1):
            left = left + residual[k] * field[k, a]
        for k in range(3):
            for c in range(2):
                lanes = slice(a * BLK + c * LANES, a * BLK + (c + 1) * LANES)
                dip_ref[k : k + 1, lanes] = moved[2 * k + c : 2 * k + c + 1, :]
                res_ref[k : k + 1, lanes] = left[2 * k + c : 2 * k + c + 1, :]


def on_device(spaces, pairs, span_y, positions, polarizability, charges, groups, pair_list, tile_count):
    atoms = positions.shape[1]
    listed = pair_list.shape[1]
    copies = len(NEAR) + SWEEPS * len(HALO) + 2 * pairs + span_y + spaces // (2 * span_y) - 3
    share = jax.ShapeDtypeStruct((3, 2 * BLK), jnp.float32)
    vmem = pl.BlockSpec(memory_space=pltpu.VMEM)
    hbm = pl.BlockSpec(memory_space=pltpu.HBM)
    return pl.pallas_call(
        functools.partial(kernel, spaces, pairs, span_y),
        out_shape=(share, share),
        in_specs=[hbm] * 5 + [pl.BlockSpec(memory_space=pltpu.SMEM)],
        out_specs=(vmem, vmem),
        scratch_shapes=[
            pltpu.VMEM((3, atoms), jnp.float32),
            pltpu.VMEM((1, atoms), jnp.float32),
            pltpu.VMEM((1, atoms), jnp.float32),
            pltpu.VMEM((1, atoms), jnp.int32),
            pltpu.VMEM((2, listed), jnp.int32),
            pltpu.VMEM((32, LANES), jnp.float32),
            pltpu.VMEM((5, 4, 3, SUBS, LANES), jnp.float32),
            pltpu.VMEM((5, 4, 2, 6, SUBS, LANES), jnp.float32),
            pltpu.VMEM((2, 5, TILES, SUBS, LANES), jnp.float32),
            pltpu.VMEM((30, SUBS, LANES), jnp.float32),
            pltpu.VMEM((60, 4, TILES, SUBS, LANES), jnp.float32),
            pltpu.VMEM((2, 3, TILES, SUBS, LANES), jnp.float32),
            pltpu.VMEM((2, 8, LANES), jnp.float32),
            pltpu.VMEM((2, 8, LANES), jnp.float32),
            pltpu.VMEM((SWEEPS + 1, 5, 4, SUBS, LANES), jnp.float32),
            pltpu.VMEM((5, 4, 6, SUBS, LANES), jnp.float32),
            pltpu.VMEM((SWEEPS, 2, 8, LANES), jnp.float32),
            pltpu.VMEM((3, 8, 16, LANES), jnp.float32),
            pltpu.SemaphoreType.DMA((5,)),
            pltpu.SemaphoreType.DMA((copies,)),
            pltpu.SemaphoreType.DMA((copies,)),
        ],
        compiler_params=pltpu.CompilerParams(
            collective_id=0, has_side_effects=True, vmem_limit_bytes=56 * 2**20
        ),
    )(
        positions,
        polarizability[None],
        charges[None],
        groups[None],
        pair_list[0].T,
        tile_count,
    )


def solution(mesh):
    spaces, pairs = mesh.shape["space"], mesh.shape["pair"]
    span_y = 8 if spaces >= 128 else 2
    return jax.shard_map(
        functools.partial(on_device, spaces, pairs, span_y),
        mesh=mesh,
        in_specs=(
            P(None, "space"),
            P("space"),
            P("space"),
            P("space"),
            P("space", None, None),
            P("space"),
        ),
        out_specs=(P(None, ("space", "pair")), P(None, ("space", "pair"))),
        check_vma=False,
    )
```

```python
import functools

import jax
import jax.numpy as jnp
from jax import lax
from jax.experimental import pallas as pl
from jax.experimental.pallas import tpu as pltpu
from jax.sharding import PartitionSpec as P

BLK = 256
BPD = 8
ITERS = 3
LANES = 128
SUBS = 8
TILES = BLK // SUBS
BUILD = 4
APPLY = 8
PERIOD = BPD * 8 * 2.15
THOLE = 0.39
ROOT_THREE = 3.0**0.5
SWEEPS = ITERS + 1
MESH = pl.DeviceIdType.MESH

NEAR = [-2, -1, 1, 2]
REACH = [-2, 2, -1, 1, 0]
TARGETS = {1: (0, 0, NEAR), 3: (0, -1, REACH), 2: (1, 0, NEAR), 0: (1, 1, REACH)}
HALO = [(column, d) for column in (1, 3, 2, 0) for d in TARGETS[column][2]]
X, Y, Z, GROUP, ROOT, CHARGE = range(6)
GRAM = [(i, j) for i in range(ITERS) for j in range(i, ITERS + 1)]


def kernel(
    spaces,
    pairs,
    span_y,
    positions_ref,
    polar_ref,
    charges_ref,
    groups_ref,
    list_ref,
    count_ref,
    dip_ref,
    res_ref,
    positions,
    polar,
    charges,
    groups,
    listing,
    flags,
    window,
    wide,
    column,
    weight,
    coef,
    cubes,
    cubed,
    acc,
    alpha,
    direct,
    vec,
    spread,
    pieces,
    field,
    gram,
    load_sem,
    send_sem,
    recv_sem,
):
    loads = [
        pltpu.make_async_copy(source, target, load_sem.at[index])
        for index, (source, target) in enumerate(
            (
                (positions_ref, positions),
                (polar_ref, polar),
                (charges_ref, charges),
                (groups_ref, groups),
                (list_ref, listing),
            )
        )
    ]
    for load in loads:
        load.start()

    sp = lax.axis_index("space")
    pr = lax.axis_index("pair")
    core = lax.rem(sp, 2)
    y = lax.rem(sp // 2, span_y)
    z = sp // (2 * span_y)
    span_z = spaces // (2 * span_y)

    def at_space(d):
        return lax.rem(sp + (d + spaces), spaces)

    def at_pair(e):
        return lax.rem(pr + (e + pairs), pairs)

    def at_core(c):
        return sp - core + lax.rem(core + c, 2)

    stages = [
        (
            [(at_core(c), at_pair(k)) for k in range(pairs) for c in range(2) if (k, c) != (0, 0)],
            pr * 2 + core,
        ),
        (
            [(sp + (lax.rem(y + k, span_y) - y) * 2, pr) for k in range(1, span_y)],
            y,
        ),
        (
            [(sp + (lax.rem(z + k, span_z) - z) * 2 * span_y, pr) for k in range(1, span_z)],
            z,
        ),
    ]

    barrier = pltpu.get_barrier_semaphore()
    partners = [(at_space(d), at_pair(e)) for d in REACH for e in (-1, 0, 1) if (d, e) != (0, 0)]
    for members, _ in stages:
        partners = partners + members
    for partner in partners:
        pl.semaphore_signal(barrier, inc=1, device_id=partner, device_id_type=MESH)

    for load in loads:
        load.wait()

    slot, partner = listing[0:1, :], listing[1:2, :]
    row_step = partner // BPD - sp
    col_step = (partner % BPD - slot + (BPD + 1)) % BPD - 1
    kind = jnp.where(row_step == 0, col_step, row_step * 3 + col_step)
    entry = lax.broadcasted_iota(jnp.int32, slot.shape, 1)
    key = jnp.where(entry < count_ref[0], kind * BPD + slot, -1)
    wanted = lax.broadcasted_iota(jnp.int32, (32, slot.shape[1]), 0)
    wanted = (wanted // 4) * BPD + (2 * pr + (BPD - 1) + wanted % 4) % BPD
    found = jnp.max((key == wanted).astype(jnp.float32), axis=1, keepdims=True)
    flags[...] = jnp.broadcast_to(found, (32, LANES))

    low = jnp.where(pr == 0, -PERIOD, 0.0).astype(jnp.float32)
    high = jnp.where(pr == pairs - 1, PERIOD, 0.0).astype(jnp.float32)
    for k in range(4):
        block = lax.rem(2 * pr + (k - 1 + BPD), BPD)
        for c in range(2):
            lanes = pl.ds(pl.multiple_of(block * BLK + c * LANES, LANES), LANES)
            shift = {0: low, 3: high}.get(k, 0.0)
            lines = {
                X: positions[0:1, lanes] + shift,
                Y: positions[1:2, lanes],
                Z: positions[2:3, lanes],
                GROUP: groups[0:1, lanes].astype(jnp.float32),
                ROOT: lax.rsqrt(polar[0:1, lanes]),
                CHARGE: charges[0:1, lanes],
            }
            for line, value in lines.items():
                window[2, k, c, line : line + 1, :] = value
            window[2, k, c, 6:8, :] = jnp.zeros((2, LANES), jnp.float32)
            if k in (1, 2):
                for m in range(3):
                    alpha[k - 1, 2 * m + c : 2 * m + c + 1, :] = polar[0:1, lanes]
        for m in range(8):
            window[2, k, 2, m : m + 1, :] = flags[4 * m + k : 4 * m + k + 1, :]

    for a in range(2):
        for c in range(2):
            turned = window[2, a + 1, c].T
            for k in (X, Y, Z, GROUP, ROOT):
                values = jnp.broadcast_to(turned[:, k : k + 1], (LANES, LANES))
                if k == ROOT:
                    values = values * -THOLE
                half = LANES // SUBS
                column[a, k, c * half : (c + 1) * half] = values.reshape(half, SUBS, LANES)
        alpha[a, 6:8, :] = jnp.zeros((2, LANES), jnp.float32)

    def widen(row, col):
        for c in range(2):
            for k in range(6):
                line = window[row, col, c, k : k + 1, :]
                wide[row, col, c, k] = jnp.broadcast_to(line, (SUBS, LANES))

    def widen_own(col, carry):
        widen(2, col)
        return carry

    def widen_rest(index, carry):
        row = index // 4
        widen(row + row // 2, index % 4)
        return carry

    pl.semaphore_wait(barrier, len(partners))

    def attr_copy(index, d):
        return pltpu.make_async_remote_copy(
            src_ref=window.at[2],
            dst_ref=window.at[2 - d],
            send_sem=send_sem.at[index],
            recv_sem=recv_sem.at[index],
            device_id=(at_space(d), pr),
            device_id_type=MESH,
        )

    for index, d in enumerate(NEAR):
        attr_copy(index, d).start()

    def weigh(a, row, step):
        slot = a * 15 + row * 3 + step
        dx = step - 1
        if row == 2:
            entry, col = (abs(dx), a + step if dx < 0 else a + 1)
        elif row > 2:
            entry, col = ((2, 5)[row - 3] + dx + 1, a + 1)
        else:
            entry, col = ((5, 2)[row] - dx + 1, a + step)
        line = window[min(row, 2), col, 2, entry : entry + 1, :]
        weight[slot, 0] = jnp.broadcast_to(line, (SUBS, LANES))
        weight[slot, 1] = jnp.broadcast_to(line * ROOT_THREE, (SUBS, LANES))

    def build(a, part, row, step, c, totals, itself, masked):
        def far(line):
            return wide[row, a + step, c, line]

        rx = column[a, X, part] - far(X)
        ry = column[a, Y, part] - far(Y)
        rz = column[a, Z, part] - far(Z)
        squared = rx * rx + ry * ry + rz * rz
        if itself:
            squared = jnp.maximum(squared, 1.0)
        inverse = lax.rsqrt(squared)
        inverse_sq = inverse * inverse
        damping = (squared * (squared * inverse)) * (column[a, ROOT, part] * far(ROOT))
        decayed = jnp.exp(damping)
        third = 1.0 - decayed
        fifth = (third + damping * decayed) * inverse
        tile = a * 15 + row * 3 + step
        three = (third * (inverse_sq * inverse)) * weight[tile, 0]
        root = (fifth * lax.rsqrt(fifth)) * (inverse_sq * weight[tile, 1])
        index = tile * 2 + c
        coef[index, 0, part] = rx * root
        coef[index, 1, part] = ry * root
        coef[index, 2, part] = rz * root
        if itself:
            shape = (BUILD, SUBS, LANES)
            own = lax.broadcasted_iota(jnp.int32, shape, 0) * SUBS + part.start * SUBS
            own = own + lax.broadcasted_iota(jnp.int32, shape, 1)
            other = lax.broadcasted_iota(jnp.int32, shape, 2) + c * LANES
            three = jnp.where(own == other, 0.0, three)
        flat = three.reshape(BUILD * SUBS, LANES)
        high = flat.astype(jnp.bfloat16)
        low = (flat - high.astype(jnp.float32)).astype(jnp.bfloat16)
        first = pl.multiple_of(part.start * SUBS, BUILD * SUBS)
        rows = pl.ds(first, BUILD * SUBS)
        lanes = pl.ds(pl.multiple_of((step * 5 + row) * LANES, LANES), LANES)
        cubes[a, 2 * c, rows, lanes] = high
        cubes[a, 2 * c + 1, rows, lanes] = low
        charged = three * far(CHARGE)
        if masked:
            charged = jnp.where(column[a, GROUP, part] != far(GROUP), charged, 0.0)
        ex, ey, ez = totals
        return (ex + charged * rx, ey + charged * ry, ez + charged * rz)

    def apply(a, part, row, step, c, totals):
        index = (a * 15 + row * 3 + step) * 2 + c
        sx, sy, sz = (coef[index, k, part] for k in range(3))
        vx, vy, vz = (spread[row, a + step, 2 * k + c] for k in range(3))
        along = sx * vx + sy * vy + sz * vz
        ex, ey, ez = totals
        return (ex + along * sx, ey + along * sy, ez + along * sz)

    def zeros(size):
        return tuple(jnp.zeros((size, SUBS, LANES), jnp.float32) for _ in range(3))

    def load_acc(a, part):
        return tuple(acc[a, k, part] for k in range(3))

    def store_acc(a, part, totals):
        for k in range(3):
            acc[a, k, part] = totals[k]

    def summed(a, with_cubes):
        if with_cubes:
            less = [
                cubed[a, c, 0:8] + cubed[a, c, 8:16] + cubed[a, c, 16:24] for c in range(2)
            ]
        parts = []
        for k in range(3):
            for c in range(2):
                half = LANES // SUBS
                turned = acc[a, k, c * half : (c + 1) * half].reshape(LANES, LANES).T
                part = jnp.sum(turned, axis=0, keepdims=True)
                if with_cubes:
                    lanes = slice(c * LANES, (c + 1) * LANES)
                    part = part - (
                        less[0][2 * k : 2 * k + 1, lanes] + less[1][2 * k + 1 : 2 * k + 2, lanes]
                    )
                parts.append(part)
        parts.append(jnp.zeros((2, LANES), jnp.float32))
        return jnp.concatenate(parts, axis=0)

    base = len(NEAR)

    def halo_copy(n, index):
        col, d = HALO[index]
        block, e, _ = TARGETS[col]
        number = base + n * len(HALO) + index
        return pltpu.make_async_remote_copy(
            src_ref=vec.at[n, 2, block + 1],
            dst_ref=vec.at[n, 2 - d, col],
            send_sem=send_sem.at[number],
            recv_sem=recv_sem.at[number],
            device_id=(at_space(d), at_pair(e)),
            device_id_type=MESH,
        )

    def send(n, block):
        for index, (col, _) in enumerate(HALO):
            if TARGETS[col][0] == block:
                halo_copy(n, index).start()

    def arrive(n, wanted_col):
        for index, (col, _) in enumerate(HALO):
            if col == wanted_col:
                halo_copy(n, index).wait()

    for a in range(2):
        for step in range(3):
            for row in (2, 3, 4):
                weigh(a, row, step)

    lax.fori_loop(0, 4, widen_own, 0)

    def build_own(group, carry):
        a = group // (TILES // BUILD)
        part = pl.ds((group - a * (TILES // BUILD)) * BUILD, BUILD)
        totals = zeros(BUILD)
        for step in range(3):
            for c in range(2):
                totals = build(a, part, 2, step, c, totals, step == 1, True)
        store_acc(a, part, totals)
        return carry

    lax.fori_loop(0, 2 * (TILES // BUILD), build_own, 0)
    for index, d in enumerate(NEAR):
        attr_copy(index, d).wait()
    for a in range(2):
        for step in range(3):
            for row in (0, 1):
                weigh(a, row, step)
    lax.fori_loop(0, 16, widen_rest, 0)

    def build_rest(a, carry):
        def one_group(group, inner):
            part = pl.ds(group * BUILD, BUILD)

            def one_row(row, totals, masked):
                for step in range(3):
                    for c in range(2):
                        totals = build(
                            a, part, row, step, c, totals, False, step == masked
                        )
                return totals

            totals = load_acc(a, part)
            totals = lax.fori_loop(0, 2, functools.partial(one_row, masked=0), totals)
            totals = lax.fori_loop(3, 5, functools.partial(one_row, masked=2), totals)
            store_acc(a, part, totals)
            return inner

        lax.fori_loop(0, TILES // BUILD, one_group, 0)
        value = summed(a, False)
        direct[a] = value
        vec[0, 2, a + 1] = value * alpha[a]
        for block in range(2):

            @pl.when(a == block)
            def _():
                send(0, block)

        return carry

    lax.fori_loop(0, 2, build_rest, 0)

    def ready(n, col):
        arrive(n, col)

        def one_row(row, carry):
            tile = vec[n, row, col]
            for m in range(6):
                spread[row, col, m] = jnp.broadcast_to(tile[m : m + 1, :], (SUBS, LANES))
            high = tile.astype(jnp.bfloat16).astype(jnp.float32)
            rest = tile - high
            middle = rest.astype(jnp.bfloat16).astype(jnp.float32)
            low = rest - middle
            parts = jnp.concatenate([high, middle, low, jnp.zeros_like(low)], axis=0)
            lanes = pl.ds(pl.multiple_of((col * 5 + row) * LANES, LANES), LANES)
            pieces[:, lanes] = parts.astype(jnp.bfloat16)
            return carry

        lax.fori_loop(0, 5, one_row, 0)

    def strips(a, steps, fresh):
        if fresh:
            cubed[a] = jnp.zeros((2, 4 * SUBS, BLK), jnp.float32)

        def one_group(group, carry):
            part = pl.ds(group * APPLY, APPLY)
            c = group // 2
            product = None
            for step in steps:
                own = pieces[:, (a + step) * 5 * LANES : (a + step + 1) * 5 * LANES]
                other = cubes[a, group, :, step * 5 * LANES : (step + 1) * 5 * LANES]
                term = lax.dot_general(
                    own,
                    other,
                    (((1,), (1,)), ((), ())),
                    preferred_element_type=jnp.float32,
                )
                product = term if product is None else product + term
            totals = zeros(APPLY) if fresh else load_acc(a, part)
            for step in steps:
                for row in range(5):
                    for k in range(2):
                        totals = apply(a, part, row, step, k, totals)
            store_acc(a, part, totals)
            cubed[a, c] = cubed[a, c] + product
            return carry

        lax.fori_loop(0, TILES // APPLY, one_group, 0)

    def finish(n, a):
        value = summed(a, True)
        field[n, a] = value
        vec[n + 1, 2, a + 1] = value * alpha[a]

        @pl.when(n + 1 < SWEEPS)
        def _():
            send(n + 1, a)

    def sweep(n, carry):
        ready(n, 1)
        strips(0, (1,), True)
        strips(1, (0,), True)
        ready(n, 2)
        ready(n, 0)
        strips(0, (0, 2), False)
        finish(n, 0)
        ready(n, 3)
        strips(1, (2, 1), False)
        finish(n, 1)
        return carry

    lax.fori_loop(0, SWEEPS, sweep, 0)

    lines = []
    for i, j in GRAM:
        product = field[i, 0] * (alpha[0] * field[j, 0]) + field[i, 1] * (alpha[1] * field[j, 1])
        lines.append(jnp.sum(product, axis=0, keepdims=True))
    lines.append(jnp.zeros((16 - len(GRAM), LANES), jnp.float32))
    total = jnp.concatenate(lines, axis=0)
    first = base + SWEEPS * len(HALO)
    for stage, (members, mine) in enumerate(stages):
        gram[stage, mine] = total
        copies = []
        for index, member in enumerate(members):
            copies.append(
                pltpu.make_async_remote_copy(
                    src_ref=gram.at[stage, mine],
                    dst_ref=gram.at[stage, mine],
                    send_sem=send_sem.at[first + index],
                    recv_sem=recv_sem.at[first + index],
                    device_id=member,
                    device_id_type=MESH,
                )
            )
            copies[-1].start()
        for copy in copies:
            copy.wait()
        first += len(members)
        total = gram[stage, 0]
        for index in range(1, len(members) + 1):
            total = total + gram[stage, index]

    sums = jnp.broadcast_to(jnp.sum(total, axis=1, keepdims=True), (16, LANES))
    entry = {}
    for index, (i, j) in enumerate(GRAM):
        entry[i, j] = entry[j, i] = sums[index : index + 1, :]

    def inner(left, right):
        value = None
        for i, u in enumerate(left):
            for j, v in enumerate(right):
                term = u * v * entry[i, j]
                value = term if value is None else value + term
        return value

    one = jnp.ones((1, LANES), jnp.float32)
    residual, direction = [one], [one]
    dipole = []
    rz_value = inner(residual, residual)
    for iteration in range(ITERS):
        size = iteration + 1
        image = [
            (direction[k] if k < size else 0.0) - (direction[k - 1] if k > 0 else 0.0)
            for k in range(size + 1)
        ]
        length = rz_value / inner(direction, image)
        dipole = [
            length * direction[k] + (dipole[k] if k < len(dipole) else 0.0) for k in range(size)
        ]
        residual = [
            (residual[k] if k < size else 0.0) - length * image[k] for k in range(size + 1)
        ]
        if iteration + 1 < ITERS:
            rz_next = inner(residual, residual)
            ratio = rz_next / rz_value
            direction = [
                residual[k] + (ratio * direction[k] if k < size else 0.0) for k in range(size + 1)
            ]
            rz_value = rz_next

    for a in range(2):
        moved = direct[a]
        for k in range(ITERS):
            moved = moved + dipole[k] * field[k, a]
        moved = moved * alpha[a]
        left = residual[0] * field[0, a]
        for k in range(1, ITERS + 1):
            left = left + residual[k] * field[k, a]
        for k in range(3):
            for c in range(2):
                lanes = slice(a * BLK + c * LANES, a * BLK + (c + 1) * LANES)
                dip_ref[k : k + 1, lanes] = moved[2 * k + c : 2 * k + c + 1, :]
                res_ref[k : k + 1, lanes] = left[2 * k + c : 2 * k + c + 1, :]


def on_device(spaces, pairs, span_y, positions, polarizability, charges, groups, pair_list, tile_count):
    atoms = positions.shape[1]
    listed = pair_list.shape[1]
    copies = len(NEAR) + SWEEPS * len(HALO) + 2 * pairs + span_y + spaces // (2 * span_y) - 3
    share = jax.ShapeDtypeStruct((3, 2 * BLK), jnp.float32)
    vmem = pl.BlockSpec(memory_space=pltpu.VMEM)
    hbm = pl.BlockSpec(memory_space=pltpu.HBM)
    return pl.pallas_call(
        functools.partial(kernel, spaces, pairs, span_y),
        out_shape=(share, share),
        in_specs=[hbm] * 5 + [pl.BlockSpec(memory_space=pltpu.SMEM)],
        out_specs=(vmem, vmem),
        scratch_shapes=[
            pltpu.VMEM((3, atoms), jnp.float32),
            pltpu.VMEM((1, atoms), jnp.float32),
            pltpu.VMEM((1, atoms), jnp.float32),
            pltpu.VMEM((1, atoms), jnp.int32),
            pltpu.VMEM((2, listed), jnp.int32),
            pltpu.VMEM((32, LANES), jnp.float32),
            pltpu.VMEM((5, 4, 3, SUBS, LANES), jnp.float32),
            pltpu.VMEM((5, 4, 2, 6, SUBS, LANES), jnp.float32),
            pltpu.VMEM((2, 5, TILES, SUBS, LANES), jnp.float32),
            pltpu.VMEM((30, 2, SUBS, LANES), jnp.float32),
            pltpu.VMEM((60, 3, TILES, SUBS, LANES), jnp.float32),
            pltpu.VMEM((2, 4, BLK, 15 * LANES), jnp.bfloat16),
            pltpu.VMEM((2, 2, 4 * SUBS, BLK), jnp.float32),
            pltpu.VMEM((2, 3, TILES, SUBS, LANES), jnp.float32),
            pltpu.VMEM((2, 8, LANES), jnp.float32),
            pltpu.VMEM((2, 8, LANES), jnp.float32),
            pltpu.VMEM((SWEEPS + 1, 5, 4, SUBS, LANES), jnp.float32),
            pltpu.VMEM((5, 4, 6, SUBS, LANES), jnp.float32),
            pltpu.VMEM((4 * SUBS, 20 * LANES), jnp.bfloat16),
            pltpu.VMEM((SWEEPS, 2, 8, LANES), jnp.float32),
            pltpu.VMEM((3, 8, 16, LANES), jnp.float32),
            pltpu.SemaphoreType.DMA((5,)),
            pltpu.SemaphoreType.DMA((copies,)),
            pltpu.SemaphoreType.DMA((copies,)),
        ],
        compiler_params=pltpu.CompilerParams(
            collective_id=0, has_side_effects=True, vmem_limit_bytes=52 * 2**20
        ),
    )(
        *[
            pltpu.with_memory_space_constraint(value, pltpu.HBM)
            for value in (
                positions,
                polarizability[None],
                charges[None],
                groups[None],
                pair_list[0].T,
            )
        ],
        tile_count,
    )


def solution(mesh):
    spaces, pairs = mesh.shape["space"], mesh.shape["pair"]
    span_y = 8 if spaces >= 128 else 2
    return jax.shard_map(
        functools.partial(on_device, spaces, pairs, span_y),
        mesh=mesh,
        in_specs=(
            P(None, "space"),
            P("space"),
            P("space"),
            P("space"),
            P("space", None, None),
            P("space"),
        ),
        out_specs=(P(None, ("space", "pair")), P(None, ("space", "pair"))),
        check_vma=False,
    )
```

```python
import functools

import jax
import jax.numpy as jnp
from jax import lax
from jax.experimental import pallas as pl
from jax.experimental.pallas import tpu as pltpu
from jax.sharding import PartitionSpec as P

BLK = 256
BPD = 8
ITERS = 3
LANES = 128
SUBS = 8
TILES = BLK // SUBS
BUILD = 4
APPLY = 8
PERIOD = BPD * 8 * 2.15
THOLE = 0.39
ROOT_THREE = 3.0**0.5
SWEEPS = ITERS + 1
MESH = pl.DeviceIdType.MESH

NEAR = [-2, -1, 1, 2]
REACH = [-2, 2, -1, 1, 0]
TARGETS = {1: (0, 0, NEAR), 3: (0, -1, REACH), 2: (1, 0, NEAR), 0: (1, 1, REACH)}
HALO = [(column, d) for column in (1, 3, 2, 0) for d in TARGETS[column][2]]
X, Y, Z, GROUP, ROOT, CHARGE = range(6)
OTHERS = (0, 1, 3, 4)
EVERY = OTHERS + (2,)
GRAM = [(i, j) for i in range(ITERS) for j in range(i, ITERS + 1)]


def kernel(
    spaces,
    pairs,
    span_y,
    positions_ref,
    polar_ref,
    charges_ref,
    groups_ref,
    list_ref,
    count_ref,
    dip_ref,
    res_ref,
    positions,
    polar,
    charges,
    groups,
    listing,
    flags,
    window,
    wide,
    column,
    weight,
    coef,
    cubes,
    cubed,
    acc,
    alpha,
    direct,
    vec,
    spread,
    pieces,
    field,
    gram,
    load_sem,
    send_sem,
    recv_sem,
):
    loads = [
        pltpu.make_async_copy(source, target, load_sem.at[index])
        for index, (source, target) in enumerate(
            (
                (positions_ref, positions),
                (polar_ref, polar),
                (charges_ref, charges),
                (groups_ref, groups),
                (list_ref, listing),
            )
        )
    ]
    for load in loads:
        load.start()

    sp = lax.axis_index("space")
    pr = lax.axis_index("pair")
    core = lax.rem(sp, 2)
    y = lax.rem(sp // 2, span_y)
    z = sp // (2 * span_y)
    span_z = spaces // (2 * span_y)

    def at_space(d):
        return lax.rem(sp + (d + spaces), spaces)

    def at_pair(e):
        return lax.rem(pr + (e + pairs), pairs)

    def at_core(c):
        return sp - core + lax.rem(core + c, 2)

    stages = [
        (
            [(at_core(c), at_pair(k)) for k in range(pairs) for c in range(2) if (k, c) != (0, 0)],
            pr * 2 + core,
        ),
        (
            [(sp + (lax.rem(y + k, span_y) - y) * 2, pr) for k in range(1, span_y)],
            y,
        ),
        (
            [(sp + (lax.rem(z + k, span_z) - z) * 2 * span_y, pr) for k in range(1, span_z)],
            z,
        ),
    ]

    barrier = pltpu.get_barrier_semaphore()
    partners = [(at_space(d), at_pair(e)) for d in REACH for e in (-1, 0, 1) if (d, e) != (0, 0)]
    for members, _ in stages:
        partners = partners + members
    for partner in partners:
        pl.semaphore_signal(barrier, inc=1, device_id=partner, device_id_type=MESH)

    for load in loads:
        load.wait()

    slot, partner = listing[0:1, :], listing[1:2, :]
    row_step = partner // BPD - sp
    col_step = (partner % BPD - slot + (BPD + 1)) % BPD - 1
    kind = jnp.where(row_step == 0, col_step, row_step * 3 + col_step)
    entry = lax.broadcasted_iota(jnp.int32, slot.shape, 1)
    key = jnp.where(entry < count_ref[0], kind * BPD + slot, -1)
    wanted = lax.broadcasted_iota(jnp.int32, (32, slot.shape[1]), 0)
    wanted = (wanted // 4) * BPD + (2 * pr + (BPD - 1) + wanted % 4) % BPD
    found = jnp.max((key == wanted).astype(jnp.float32), axis=1, keepdims=True)
    flags[...] = jnp.broadcast_to(found, (32, LANES))

    low = jnp.where(pr == 0, -PERIOD, 0.0).astype(jnp.float32)
    high = jnp.where(pr == pairs - 1, PERIOD, 0.0).astype(jnp.float32)
    for k in range(4):
        block = lax.rem(2 * pr + (k - 1 + BPD), BPD)
        for c in range(2):
            lanes = pl.ds(pl.multiple_of(block * BLK + c * LANES, LANES), LANES)
            shift = {0: low, 3: high}.get(k, 0.0)
            lines = {
                X: positions[0:1, lanes] + shift,
                Y: positions[1:2, lanes],
                Z: positions[2:3, lanes],
                GROUP: groups[0:1, lanes].astype(jnp.float32),
                ROOT: lax.rsqrt(polar[0:1, lanes]),
                CHARGE: charges[0:1, lanes],
            }
            for line, value in lines.items():
                window[2, k, c, line : line + 1, :] = value
            window[2, k, c, 6:8, :] = jnp.zeros((2, LANES), jnp.float32)
            if k in (1, 2):
                for m in range(3):
                    alpha[k - 1, 2 * m + c : 2 * m + c + 1, :] = polar[0:1, lanes]
        for m in range(8):
            window[2, k, 2, m : m + 1, :] = flags[4 * m + k : 4 * m + k + 1, :]

    for a in range(2):
        for c in range(2):
            turned = window[2, a + 1, c].T
            for k in (X, Y, Z, GROUP, ROOT):
                values = jnp.broadcast_to(turned[:, k : k + 1], (LANES, LANES))
                if k == ROOT:
                    values = values * -THOLE
                half = LANES // SUBS
                column[a, k, c * half : (c + 1) * half] = values.reshape(half, SUBS, LANES)
        alpha[a, 6:8, :] = jnp.zeros((2, LANES), jnp.float32)

    def place(row):
        if isinstance(row, int) and row == 2:
            return 4
        return row - row // 3 if isinstance(row, int) else row - lax.div(row, 3)

    def widen(row, col):
        for c in range(2):
            for k in range(6):
                line = window[row, col, c, k : k + 1, :]
                wide[row, col, c, k] = jnp.broadcast_to(line, (SUBS, LANES))

    def widen_own(col, carry):
        widen(2, col)
        return carry

    def widen_rest(index, carry):
        row = index // 4
        widen(row + row // 2, index % 4)
        return carry

    pl.semaphore_wait(barrier, len(partners))

    def attr_copy(index, d):
        return pltpu.make_async_remote_copy(
            src_ref=window.at[2],
            dst_ref=window.at[2 - d],
            send_sem=send_sem.at[index],
            recv_sem=recv_sem.at[index],
            device_id=(at_space(d), pr),
            device_id_type=MESH,
        )

    for index, d in enumerate(NEAR):
        attr_copy(index, d).start()

    def weigh(a, row, step):
        slot = a * 15 + row * 3 + step
        dx = step - 1
        if row == 2:
            entry, col = (abs(dx), a + step if dx < 0 else a + 1)
        elif row > 2:
            entry, col = ((2, 5)[row - 3] + dx + 1, a + 1)
        else:
            entry, col = ((5, 2)[row] - dx + 1, a + step)
        line = window[min(row, 2), col, 2, entry : entry + 1, :]
        weight[slot, 0] = jnp.broadcast_to(line, (SUBS, LANES))
        weight[slot, 1] = jnp.broadcast_to(line * ROOT_THREE, (SUBS, LANES))

    def build(a, part, row, step, c, totals, itself, masked):
        def far(line):
            return wide[row, a + step, c, line]

        rx = column[a, X, part] - far(X)
        ry = column[a, Y, part] - far(Y)
        rz = column[a, Z, part] - far(Z)
        squared = rx * rx + ry * ry + rz * rz
        if itself:
            squared = jnp.maximum(squared, 1.0)
        inverse = lax.rsqrt(squared)
        inverse_sq = inverse * inverse
        damping = (squared * (squared * inverse)) * (column[a, ROOT, part] * far(ROOT))
        decayed = jnp.exp(damping)
        third = 1.0 - decayed
        fifth = (third + damping * decayed) * inverse
        tile = a * 15 + row * 3 + step
        three = (third * (inverse_sq * inverse)) * weight[tile, 0]
        root = (fifth * lax.rsqrt(fifth)) * (inverse_sq * weight[tile, 1])
        index = tile * 2 + c
        coef[index, 0, part] = rx * root
        coef[index, 1, part] = ry * root
        coef[index, 2, part] = rz * root
        if itself:
            shape = (BUILD, SUBS, LANES)
            own = lax.broadcasted_iota(jnp.int32, shape, 0) * SUBS + part.start * SUBS
            own = own + lax.broadcasted_iota(jnp.int32, shape, 1)
            other = lax.broadcasted_iota(jnp.int32, shape, 2) + c * LANES
            three = jnp.where(own == other, 0.0, three)
        flat = three.reshape(BUILD * SUBS, LANES)
        high = flat.astype(jnp.bfloat16)
        low = (flat - high.astype(jnp.float32)).astype(jnp.bfloat16)
        first = pl.multiple_of(part.start * SUBS, BUILD * SUBS)
        rows = pl.ds(first, BUILD * SUBS)
        lanes = pl.ds(pl.multiple_of((step * 5 + place(row)) * LANES, LANES), LANES)
        cubes[a, 2 * c, rows, lanes] = high
        cubes[a, 2 * c + 1, rows, lanes] = low
        charged = three * far(CHARGE)
        if masked:
            charged = jnp.where(column[a, GROUP, part] != far(GROUP), charged, 0.0)
        ex, ey, ez = totals
        return (ex + charged * rx, ey + charged * ry, ez + charged * rz)

    def apply(a, part, row, step, c, totals):
        index = (a * 15 + row * 3 + step) * 2 + c
        sx, sy, sz = (coef[index, k, part] for k in range(3))
        vx, vy, vz = (spread[row, a + step, 2 * k + c] for k in range(3))
        along = sx * vx + sy * vy + sz * vz
        ex, ey, ez = totals
        return (ex + along * sx, ey + along * sy, ez + along * sz)

    def zeros(size):
        return tuple(jnp.zeros((size, SUBS, LANES), jnp.float32) for _ in range(3))

    def load_acc(a, part):
        return tuple(acc[a, k, part] for k in range(3))

    def store_acc(a, part, totals):
        for k in range(3):
            acc[a, k, part] = totals[k]

    def summed(a, with_cubes):
        if with_cubes:
            less = [
                cubed[a, c, 0:8] + cubed[a, c, 8:16] + cubed[a, c, 16:24] for c in range(2)
            ]
        parts = []
        for k in range(3):
            for c in range(2):
                half = LANES // SUBS
                turned = acc[a, k, c * half : (c + 1) * half].reshape(LANES, LANES).T
                part = jnp.sum(turned, axis=0, keepdims=True)
                if with_cubes:
                    lanes = slice(c * LANES, (c + 1) * LANES)
                    part = part - (
                        less[0][2 * k : 2 * k + 1, lanes] + less[1][2 * k + 1 : 2 * k + 2, lanes]
                    )
                parts.append(part)
        parts.append(jnp.zeros((2, LANES), jnp.float32))
        return jnp.concatenate(parts, axis=0)

    base = len(NEAR)

    def halo_copy(n, index):
        col, d = HALO[index]
        block, e, _ = TARGETS[col]
        number = base + n * len(HALO) + index
        return pltpu.make_async_remote_copy(
            src_ref=vec.at[n, 2, block + 1],
            dst_ref=vec.at[n, 2 - d, col],
            send_sem=send_sem.at[number],
            recv_sem=recv_sem.at[number],
            device_id=(at_space(d), at_pair(e)),
            device_id_type=MESH,
        )

    def send(n, block):
        for index, (col, _) in enumerate(HALO):
            if TARGETS[col][0] == block:
                halo_copy(n, index).start()

    for a in range(2):
        for step in range(3):
            for row in (2, 3, 4):
                weigh(a, row, step)

    lax.fori_loop(0, 4, widen_own, 0)

    def build_own(group, carry):
        a = group // (TILES // BUILD)
        part = pl.ds((group - a * (TILES // BUILD)) * BUILD, BUILD)
        totals = zeros(BUILD)
        for step in range(3):
            for c in range(2):
                totals = build(a, part, 2, step, c, totals, step == 1, True)
        store_acc(a, part, totals)
        return carry

    lax.fori_loop(0, 2 * (TILES // BUILD), build_own, 0)
    for index, d in enumerate(NEAR):
        attr_copy(index, d).wait()
    for a in range(2):
        for step in range(3):
            for row in (0, 1):
                weigh(a, row, step)
    lax.fori_loop(0, 16, widen_rest, 0)

    def build_rest(a, carry):
        def one_group(group, inner):
            part = pl.ds(group * BUILD, BUILD)

            def one_row(row, totals, masked):
                for step in range(3):
                    for c in range(2):
                        totals = build(
                            a, part, row, step, c, totals, False, step == masked
                        )
                return totals

            totals = load_acc(a, part)
            totals = lax.fori_loop(0, 2, functools.partial(one_row, masked=0), totals)
            totals = lax.fori_loop(3, 5, functools.partial(one_row, masked=2), totals)
            store_acc(a, part, totals)
            return inner

        lax.fori_loop(0, TILES // BUILD, one_group, 0)
        value = summed(a, False)
        direct[a] = value
        vec[0, 2, a + 1] = value * alpha[a]
        for block in range(2):

            @pl.when(a == block)
            def _():
                send(0, block)

        return carry

    lax.fori_loop(0, 2, build_rest, 0)

    def take(n, row, col):
        tile = vec[n, row, col]
        for m in range(6):
            spread[row, col, m] = jnp.broadcast_to(tile[m : m + 1, :], (SUBS, LANES))
        high = tile.astype(jnp.bfloat16).astype(jnp.float32)
        rest = tile - high
        middle = rest.astype(jnp.bfloat16).astype(jnp.float32)
        low = rest - middle
        parts = jnp.concatenate([high, middle, low, jnp.zeros_like(low)], axis=0)
        lanes = pl.ds((col * 5 + place(row)) * LANES, LANES)
        pieces[:, lanes] = parts.astype(jnp.bfloat16)

    def ready(n, col):
        for index, (far, d) in enumerate(HALO):
            if far == col:
                halo_copy(n, index).wait()
                take(n, 2 - d, col)

    def strips(a, steps, rows, fresh):
        first, last = (place(rows[0]), place(rows[-1]) + 1)
        if fresh:
            cubed[a] = jnp.zeros((2, 4 * SUBS, BLK), jnp.float32)

        def one_group(group, carry):
            part = pl.ds(group * APPLY, APPLY)
            c = group // 2
            product = None
            for step in steps:
                own = (a + step) * 5
                term = lax.dot_general(
                    pieces[:, (own + first) * LANES : (own + last) * LANES],
                    cubes[
                        a, group, :, (step * 5 + first) * LANES : (step * 5 + last) * LANES
                    ],
                    (((1,), (1,)), ((), ())),
                    preferred_element_type=jnp.float32,
                )
                product = term if product is None else product + term
            totals = zeros(APPLY) if fresh else load_acc(a, part)
            for step in steps:
                for row in rows:
                    for k in range(2):
                        totals = apply(a, part, row, step, k, totals)
            store_acc(a, part, totals)
            cubed[a, c] = cubed[a, c] + product
            return carry

        lax.fori_loop(0, TILES // APPLY, one_group, 0)

    def finish(n, a):
        value = summed(a, True)
        field[n, a] = value
        vec[n + 1, 2, a + 1] = value * alpha[a]

        @pl.when(n + 1 < SWEEPS)
        def _():
            send(n + 1, a)

    def sweep(n, carry):
        take(n, 2, 1)
        take(n, 2, 2)
        strips(0, (1, 2), (2,), True)
        strips(1, (0, 1), (2,), True)
        ready(n, 1)
        strips(0, (1,), OTHERS, False)
        strips(1, (0,), OTHERS, False)
        ready(n, 2)
        strips(1, (1,), OTHERS, False)
        strips(0, (2,), OTHERS, False)
        ready(n, 0)
        strips(0, (0,), EVERY, False)
        finish(n, 0)
        ready(n, 3)
        strips(1, (2,), EVERY, False)
        finish(n, 1)
        return carry

    lax.fori_loop(0, SWEEPS, sweep, 0)

    lines = []
    for i, j in GRAM:
        product = field[i, 0] * (alpha[0] * field[j, 0]) + field[i, 1] * (alpha[1] * field[j, 1])
        lines.append(jnp.sum(product, axis=0, keepdims=True))
    lines.append(jnp.zeros((16 - len(GRAM), LANES), jnp.float32))
    total = jnp.concatenate(lines, axis=0)
    first = base + SWEEPS * len(HALO)
    for stage, (members, mine) in enumerate(stages):
        gram[stage, mine] = total
        copies = []
        for index, member in enumerate(members):
            copies.append(
                pltpu.make_async_remote_copy(
                    src_ref=gram.at[stage, mine],
                    dst_ref=gram.at[stage, mine],
                    send_sem=send_sem.at[first + index],
                    recv_sem=recv_sem.at[first + index],
                    device_id=member,
                    device_id_type=MESH,
                )
            )
            copies[-1].start()
        for copy in copies:
            copy.wait()
        first += len(members)
        total = gram[stage, 0]
        for index in range(1, len(members) + 1):
            total = total + gram[stage, index]

    sums = jnp.broadcast_to(jnp.sum(total, axis=1, keepdims=True), (16, LANES))
    entry = {}
    for index, (i, j) in enumerate(GRAM):
        entry[i, j] = entry[j, i] = sums[index : index + 1, :]

    def inner(left, right):
        value = None
        for i, u in enumerate(left):
            for j, v in enumerate(right):
                term = u * v * entry[i, j]
                value = term if value is None else value + term
        return value

    one = jnp.ones((1, LANES), jnp.float32)
    residual, direction = [one], [one]
    dipole = []
    rz_value = inner(residual, residual)
    for iteration in range(ITERS):
        size = iteration + 1
        image = [
            (direction[k] if k < size else 0.0) - (direction[k - 1] if k > 0 else 0.0)
            for k in range(size + 1)
        ]
        length = rz_value / inner(direction, image)
        dipole = [
            length * direction[k] + (dipole[k] if k < len(dipole) else 0.0) for k in range(size)
        ]
        residual = [
            (residual[k] if k < size else 0.0) - length * image[k] for k in range(size + 1)
        ]
        if iteration + 1 < ITERS:
            rz_next = inner(residual, residual)
            ratio = rz_next / rz_value
            direction = [
                residual[k] + (ratio * direction[k] if k < size else 0.0) for k in range(size + 1)
            ]
            rz_value = rz_next

    for a in range(2):
        moved = direct[a]
        for k in range(ITERS):
            moved = moved + dipole[k] * field[k, a]
        moved = moved * alpha[a]
        left = residual[0] * field[0, a]
        for k in range(1, ITERS + 1):
            left = left + residual[k] * field[k, a]
        for k in range(3):
            for c in range(2):
                lanes = slice(a * BLK + c * LANES, a * BLK + (c + 1) * LANES)
                dip_ref[k : k + 1, lanes] = moved[2 * k + c : 2 * k + c + 1, :]
                res_ref[k : k + 1, lanes] = left[2 * k + c : 2 * k + c + 1, :]


def on_device(spaces, pairs, span_y, positions, polarizability, charges, groups, pair_list, tile_count):
    atoms = positions.shape[1]
    listed = pair_list.shape[1]
    copies = len(NEAR) + SWEEPS * len(HALO) + 2 * pairs + span_y + spaces // (2 * span_y) - 3
    share = jax.ShapeDtypeStruct((3, 2 * BLK), jnp.float32)
    vmem = pl.BlockSpec(memory_space=pltpu.VMEM)
    hbm = pl.BlockSpec(memory_space=pltpu.HBM)
    return pl.pallas_call(
        functools.partial(kernel, spaces, pairs, span_y),
        out_shape=(share, share),
        in_specs=[hbm] * 5 + [pl.BlockSpec(memory_space=pltpu.SMEM)],
        out_specs=(vmem, vmem),
        scratch_shapes=[
            pltpu.VMEM((3, atoms), jnp.float32),
            pltpu.VMEM((1, atoms), jnp.float32),
            pltpu.VMEM((1, atoms), jnp.float32),
            pltpu.VMEM((1, atoms), jnp.int32),
            pltpu.VMEM((2, listed), jnp.int32),
            pltpu.VMEM((32, LANES), jnp.float32),
            pltpu.VMEM((5, 4, 3, SUBS, LANES), jnp.float32),
            pltpu.VMEM((5, 4, 2, 6, SUBS, LANES), jnp.float32),
            pltpu.VMEM((2, 5, TILES, SUBS, LANES), jnp.float32),
            pltpu.VMEM((30, 2, SUBS, LANES), jnp.float32),
            pltpu.VMEM((60, 3, TILES, SUBS, LANES), jnp.float32),
            pltpu.VMEM((2, 4, BLK, 15 * LANES), jnp.bfloat16),
            pltpu.VMEM((2, 2, 4 * SUBS, BLK), jnp.float32),
            pltpu.VMEM((2, 3, TILES, SUBS, LANES), jnp.float32),
            pltpu.VMEM((2, 8, LANES), jnp.float32),
            pltpu.VMEM((2, 8, LANES), jnp.float32),
            pltpu.VMEM((SWEEPS + 1, 5, 4, SUBS, LANES), jnp.float32),
            pltpu.VMEM((5, 4, 6, SUBS, LANES), jnp.float32),
            pltpu.VMEM((4 * SUBS, 20 * LANES), jnp.bfloat16),
            pltpu.VMEM((SWEEPS, 2, 8, LANES), jnp.float32),
            pltpu.VMEM((3, 8, 16, LANES), jnp.float32),
            pltpu.SemaphoreType.DMA((5,)),
            pltpu.SemaphoreType.DMA((copies,)),
            pltpu.SemaphoreType.DMA((copies,)),
        ],
        compiler_params=pltpu.CompilerParams(
            collective_id=0, has_side_effects=True, vmem_limit_bytes=52 * 2**20
        ),
    )(
        *[
            pltpu.with_memory_space_constraint(value, pltpu.HBM)
            for value in (
                positions,
                polarizability[None],
                charges[None],
                groups[None],
                pair_list[0].T,
            )
        ],
        tile_count,
    )


def solution(mesh):
    spaces, pairs = mesh.shape["space"], mesh.shape["pair"]
    span_y = 8 if spaces >= 128 else 2
    return jax.shard_map(
        functools.partial(on_device, spaces, pairs, span_y),
        mesh=mesh,
        in_specs=(
            P(None, "space"),
            P("space"),
            P("space"),
            P("space"),
            P("space", None, None),
            P("space"),
        ),
        out_specs=(P(None, ("space", "pair")), P(None, ("space", "pair"))),
        check_vma=False,
    )
```

```python
import functools

import jax
import jax.numpy as jnp
from jax import lax
from jax.experimental import pallas as pl
from jax.experimental.pallas import tpu as pltpu
from jax.sharding import PartitionSpec as P

BLK = 256
BPD = 8
ITERS = 3
LANES = 128
SUBS = 8
TILES = BLK // SUBS
BUILD = 4
APPLY = 8
PERIOD = BPD * 8 * 2.15
THOLE = 0.39
ROOT_THREE = 3.0**0.5
SWEEPS = ITERS + 1
MESH = pl.DeviceIdType.MESH

NEAR = [-2, -1, 1, 2]
REACH = [-2, 2, -1, 1, 0]
TARGETS = {1: (0, 0, NEAR), 3: (0, -1, REACH), 2: (1, 0, NEAR), 0: (1, 1, REACH)}
HALO = [(column, d) for column in (1, 3, 2, 0) for d in TARGETS[column][2]]
X, Y, Z, GROUP, ROOT, CHARGE = range(6)
OTHERS = (0, 1, 3, 4)
EVERY = OTHERS + (2,)
DISTANT = (0, 4)
GRAM = [(i, j) for i in range(ITERS) for j in range(i, ITERS + 1)]


def kernel(
    spaces,
    pairs,
    span_y,
    positions_ref,
    polar_ref,
    charges_ref,
    groups_ref,
    list_ref,
    count_ref,
    dip_ref,
    res_ref,
    positions,
    polar,
    charges,
    groups,
    listing,
    flags,
    window,
    wide,
    column,
    weight,
    coef,
    cubes,
    cubed,
    fives,
    fived,
    apart,
    centred,
    moments,
    acc,
    alpha,
    direct,
    vec,
    spread,
    pieces,
    field,
    gram,
    load_sem,
    send_sem,
    recv_sem,
):
    loads = [
        pltpu.make_async_copy(source, target, load_sem.at[index])
        for index, (source, target) in enumerate(
            (
                (positions_ref, positions),
                (polar_ref, polar),
                (charges_ref, charges),
                (groups_ref, groups),
                (list_ref, listing),
            )
        )
    ]
    for load in loads:
        load.start()

    sp = lax.axis_index("space")
    pr = lax.axis_index("pair")
    core = lax.rem(sp, 2)
    y = lax.rem(sp // 2, span_y)
    z = sp // (2 * span_y)
    span_z = spaces // (2 * span_y)

    def at_space(d):
        return lax.rem(sp + (d + spaces), spaces)

    def at_pair(e):
        return lax.rem(pr + (e + pairs), pairs)

    def at_core(c):
        return sp - core + lax.rem(core + c, 2)

    stages = [
        (
            [(at_core(c), at_pair(k)) for k in range(pairs) for c in range(2) if (k, c) != (0, 0)],
            pr * 2 + core,
        ),
        (
            [(sp + (lax.rem(y + k, span_y) - y) * 2, pr) for k in range(1, span_y)],
            y,
        ),
        (
            [(sp + (lax.rem(z + k, span_z) - z) * 2 * span_y, pr) for k in range(1, span_z)],
            z,
        ),
    ]

    barrier = pltpu.get_barrier_semaphore()
    partners = [(at_space(d), at_pair(e)) for d in REACH for e in (-1, 0, 1) if (d, e) != (0, 0)]
    for members, _ in stages:
        partners = partners + members
    for partner in partners:
        pl.semaphore_signal(barrier, inc=1, device_id=partner, device_id_type=MESH)

    for load in loads:
        load.wait()

    slot, partner = listing[0:1, :], listing[1:2, :]
    row_step = partner // BPD - sp
    col_step = (partner % BPD - slot + (BPD + 1)) % BPD - 1
    kind = jnp.where(row_step == 0, col_step, row_step * 3 + col_step)
    entry = lax.broadcasted_iota(jnp.int32, slot.shape, 1)
    key = jnp.where(entry < count_ref[0], kind * BPD + slot, -1)
    wanted = lax.broadcasted_iota(jnp.int32, (32, slot.shape[1]), 0)
    wanted = (wanted // 4) * BPD + (2 * pr + (BPD - 1) + wanted % 4) % BPD
    found = jnp.max((key == wanted).astype(jnp.float32), axis=1, keepdims=True)
    flags[...] = jnp.broadcast_to(found, (32, LANES))

    low = jnp.where(pr == 0, -PERIOD, 0.0).astype(jnp.float32)
    high = jnp.where(pr == pairs - 1, PERIOD, 0.0).astype(jnp.float32)
    for k in range(4):
        block = lax.rem(2 * pr + (k - 1 + BPD), BPD)
        for c in range(2):
            lanes = pl.ds(pl.multiple_of(block * BLK + c * LANES, LANES), LANES)
            shift = {0: low, 3: high}.get(k, 0.0)
            lines = {
                X: positions[0:1, lanes] + shift,
                Y: positions[1:2, lanes],
                Z: positions[2:3, lanes],
                GROUP: groups[0:1, lanes].astype(jnp.float32),
                ROOT: lax.rsqrt(polar[0:1, lanes]),
                CHARGE: charges[0:1, lanes],
            }
            for line, value in lines.items():
                window[2, k, c, line : line + 1, :] = value
            window[2, k, c, 6:8, :] = jnp.zeros((2, LANES), jnp.float32)
            if k in (1, 2):
                for m in range(3):
                    alpha[k - 1, 2 * m + c : 2 * m + c + 1, :] = polar[0:1, lanes]
        for m in range(8):
            window[2, k, 2, m : m + 1, :] = flags[4 * m + k : 4 * m + k + 1, :]

    def place(row):
        return EVERY.index(row)

    def widen(row, col):
        for c in range(2):
            for k in range(6):
                line = window[row, col, c, k : k + 1, :]
                wide[row, col, c, k] = jnp.broadcast_to(line, (SUBS, LANES))

    def widen_own(col, carry):
        widen(2, col)
        return carry

    def widen_rest(index, carry):
        row = index // 4
        widen(row + row // 2, index % 4)
        return carry

    pl.semaphore_wait(barrier, len(partners))

    def attr_copy(index, d):
        return pltpu.make_async_remote_copy(
            src_ref=window.at[2],
            dst_ref=window.at[2 - d],
            send_sem=send_sem.at[index],
            recv_sem=recv_sem.at[index],
            device_id=(at_space(d), pr),
            device_id_type=MESH,
        )

    for index, d in enumerate(NEAR):
        attr_copy(index, d).start()

    for a in range(2):
        for c in range(2):
            turned = window[2, a + 1, c].T
            for k in (X, Y, Z, GROUP, ROOT):
                values = jnp.broadcast_to(turned[:, k : k + 1], (LANES, LANES))
                if k == ROOT:
                    values = values * -THOLE
                half = LANES // SUBS
                column[a, k, c * half : (c + 1) * half] = values.reshape(half, SUBS, LANES)
        alpha[a, 6:8, :] = jnp.zeros((2, LANES), jnp.float32)

    sublane = lax.broadcasted_iota(jnp.int32, (SUBS, LANES), 0)
    fourth = lax.rem(sublane, 4)

    def choose(x, y, z, other):
        return jnp.where(
            fourth == 0, x, jnp.where(fourth == 1, y, jnp.where(fourth == 2, z, other))
        )

    def centre(a):
        mean = jnp.sum(window[2, a + 1, 0] + window[2, a + 1, 1], axis=1, keepdims=True) / BLK
        return [jnp.broadcast_to(mean[k : k + 1, :], (SUBS, LANES)) for k in range(3)]

    def set_apart():
        for a in range(2):
            middle = centre(a)
            for step in range(3):
                for index, row in enumerate(DISTANT):
                    for c in range(2):
                        for k in range(3):
                            apart[a, step, index, c, k] = wide[row, a + step, c, k] - middle[k]
            for c in range(2):
                own = [wide[2, a + 1, c, k] - middle[k] for k in range(3)]
                centred[a, c] = choose(*own, -1.0)

    def weigh(a, row, step):
        slot = a * 15 + row * 3 + step
        dx = step - 1
        if row == 2:
            entry, col = (abs(dx), a + step if dx < 0 else a + 1)
        elif row > 2:
            entry, col = ((2, 5)[row - 3] + dx + 1, a + 1)
        else:
            entry, col = ((5, 2)[row] - dx + 1, a + step)
        line = window[min(row, 2), col, 2, entry : entry + 1, :]
        weight[slot, 0] = jnp.broadcast_to(line, (SUBS, LANES))
        weight[slot, 1] = jnp.broadcast_to(line * ROOT_THREE, (SUBS, LANES))
        weight[slot, 2] = jnp.broadcast_to(line * 3.0, (SUBS, LANES))

    def build(a, part, row, step, c, totals, itself, masked):
        def far(line):
            return wide[row, a + step, c, line]

        rx = column[a, X, part] - far(X)
        ry = column[a, Y, part] - far(Y)
        rz = column[a, Z, part] - far(Z)
        squared = rx * rx + ry * ry + rz * rz
        if itself:
            squared = jnp.maximum(squared, 1.0)
        inverse = lax.rsqrt(squared)
        inverse_sq = inverse * inverse
        damping = (squared * (squared * inverse)) * (column[a, ROOT, part] * far(ROOT))
        decayed = jnp.exp(damping)
        third = 1.0 - decayed
        fifth = (third + damping * decayed) * inverse
        tile = a * 15 + row * 3 + step
        three = (third * (inverse_sq * inverse)) * weight[tile, 0]
        rows = pl.ds(pl.multiple_of(part.start * SUBS, BUILD * SUBS), BUILD * SUBS)

        def keep(matrices, value, lanes):
            flat = value.reshape(BUILD * SUBS, LANES)
            high = flat.astype(jnp.bfloat16)
            low = (flat - high.astype(jnp.float32)).astype(jnp.bfloat16)
            matrices[a, 2 * c, rows, lanes] = high
            matrices[a, 2 * c + 1, rows, lanes] = low

        if row in DISTANT:
            five = (fifth * (inverse_sq * inverse_sq)) * weight[tile, 2]
            lane = (step * 2 + DISTANT.index(row)) * LANES
            keep(fives, five, slice(lane, lane + LANES))
        else:
            root = (fifth * lax.rsqrt(fifth)) * (inverse_sq * weight[tile, 1])
            index = tile * 2 + c
            coef[index, 0, part] = rx * root
            coef[index, 1, part] = ry * root
            coef[index, 2, part] = rz * root
        if itself:
            shape = (BUILD, SUBS, LANES)
            own = lax.broadcasted_iota(jnp.int32, shape, 0) * SUBS + part.start * SUBS
            own = own + lax.broadcasted_iota(jnp.int32, shape, 1)
            other = lax.broadcasted_iota(jnp.int32, shape, 2) + c * LANES
            three = jnp.where(own == other, 0.0, three)
        lane = (step * 5 + place(row)) * LANES
        keep(cubes, three, slice(lane, lane + LANES))
        charged = three * far(CHARGE)
        if masked:
            charged = jnp.where(column[a, GROUP, part] != far(GROUP), charged, 0.0)
        ex, ey, ez = totals
        return (ex + charged * rx, ey + charged * ry, ez + charged * rz)

    def apply(a, part, row, step, c, totals):
        index = (a * 15 + row * 3 + step) * 2 + c
        sx, sy, sz = (coef[index, k, part] for k in range(3))
        vx, vy, vz = (spread[row, a + step, 2 * k + c] for k in range(3))
        along = sx * vx + sy * vy + sz * vz
        ex, ey, ez = totals
        return (ex + along * sx, ey + along * sy, ez + along * sz)

    def zeros(size):
        return tuple(jnp.zeros((size, SUBS, LANES), jnp.float32) for _ in range(3))

    def load_acc(a, part):
        return tuple(acc[a, k, part] for k in range(3))

    def store_acc(a, part, totals):
        for k in range(3):
            acc[a, k, part] = totals[k]

    def summed(a, with_cubes):
        if with_cubes:
            less = [
                cubed[a, c, 0:8] + cubed[a, c, 8:16] + cubed[a, c, 16:24] for c in range(2)
            ]
            expanded = []
            for c in range(2):
                lanes = slice(c * LANES, (c + 1) * LANES)
                sums = []
                for half in range(2):
                    first = half * SUBS
                    piece = [fived[a, first + 16 * m : first + 16 * m + 8, lanes] for m in range(3)]
                    terms = (piece[0] + piece[1] + piece[2]) * centred[a, c]
                    for quarter in range(2):
                        rows = terms[4 * quarter : 4 * quarter + 4, :]
                        sums.append(jnp.sum(rows, axis=0, keepdims=True))
                expanded.append(sums)
        parts = []
        for k in range(3):
            for c in range(2):
                half = LANES // SUBS
                turned = acc[a, k, c * half : (c + 1) * half].reshape(LANES, LANES).T
                part = jnp.sum(turned, axis=0, keepdims=True)
                if with_cubes:
                    lanes = slice(c * LANES, (c + 1) * LANES)
                    part = part - (
                        less[0][2 * k : 2 * k + 1, lanes] + less[1][2 * k + 1 : 2 * k + 2, lanes]
                    )
                    own = centred[a, c][k : k + 1, :]
                    part = part + (own * expanded[c][0] - expanded[c][k + 1])
                parts.append(part)
        parts.append(jnp.zeros((2, LANES), jnp.float32))
        return jnp.concatenate(parts, axis=0)

    base = len(NEAR)

    def halo_copy(n, index):
        col, d = HALO[index]
        block, e, _ = TARGETS[col]
        number = base + n * len(HALO) + index
        return pltpu.make_async_remote_copy(
            src_ref=vec.at[n, 2, block + 1],
            dst_ref=vec.at[n, 2 - d, col],
            send_sem=send_sem.at[number],
            recv_sem=recv_sem.at[number],
            device_id=(at_space(d), at_pair(e)),
            device_id_type=MESH,
        )

    def send(n, block):
        for index, (col, _) in enumerate(HALO):
            if TARGETS[col][0] == block:
                halo_copy(n, index).start()

    for a in range(2):
        for step in range(3):
            for row in (2, 3, 4):
                weigh(a, row, step)

    lax.fori_loop(0, 4, widen_own, 0)

    def build_own(group, carry):
        a = group // (TILES // BUILD)
        part = pl.ds((group - a * (TILES // BUILD)) * BUILD, BUILD)
        totals = zeros(BUILD)
        for step in range(3):
            for c in range(2):
                totals = build(a, part, 2, step, c, totals, step == 1, True)
        store_acc(a, part, totals)
        return carry

    lax.fori_loop(0, 2 * (TILES // BUILD), build_own, 0)
    for index, d in enumerate(NEAR):
        attr_copy(index, d).wait()
    for a in range(2):
        for step in range(3):
            for row in (0, 1):
                weigh(a, row, step)
    lax.fori_loop(0, 16, widen_rest, 0)
    set_apart()

    def build_rest(a, carry):
        def one_group(group, inner):
            part = pl.ds(group * BUILD, BUILD)

            totals = load_acc(a, part)
            for row in OTHERS:
                for step in range(3):
                    for c in range(2):
                        masked = (row, step) in ((1, 0), (3, 2))
                        totals = build(a, part, row, step, c, totals, False, masked)
            store_acc(a, part, totals)
            return inner

        lax.fori_loop(0, TILES // BUILD, one_group, 0)
        value = summed(a, False)
        direct[a] = value
        vec[0, 2, a + 1] = value * alpha[a]
        for block in range(2):

            @pl.when(a == block)
            def _():
                send(0, block)

        return carry

    lax.fori_loop(0, 2, build_rest, 0)

    def thirds(value):
        high = value.astype(jnp.bfloat16).astype(jnp.float32)
        rest = value - high
        middle = rest.astype(jnp.bfloat16).astype(jnp.float32)
        return [high, middle, rest - middle]

    def take(n, row, col):
        tile = vec[n, row, col]
        lines = [jnp.broadcast_to(tile[m : m + 1, :], (SUBS, LANES)) for m in range(6)]
        parts = jnp.concatenate(thirds(tile) + [jnp.zeros_like(tile)], axis=0)
        lane = (col * 5 + place(row)) * LANES
        pieces[:, lane : lane + LANES] = parts.astype(jnp.bfloat16)
        if row not in DISTANT:
            for m in range(6):
                spread[row, col, m] = lines[m]
            return
        index = DISTANT.index(row)
        for a in range(2):
            step = col - a
            if not 0 <= step < 3:
                continue
            for c in range(2):
                x, y, z = (apart[a, step, index, c, k] for k in range(3))
                vx, vy, vz = (lines[2 * k + c] for k in range(3))
                four = choose(vx, vy, vz, x * vx + y * vy + z * vz)
                upper = four * jnp.where(sublane < 4, 1.0, x)
                lower = four * jnp.where(sublane < 4, y, z)
                uppers, lowers = thirds(upper), thirds(lower)
                parts = [value for pair in zip(uppers, lowers) for value in pair]
                lane = (step * 2 + index) * LANES
                moments[a, c, :, lane : lane + LANES] = jnp.concatenate(parts, axis=0).astype(
                    jnp.bfloat16
                )

    def ready(n, col):
        for index, (far, d) in enumerate(HALO):
            if far == col:
                halo_copy(n, index).wait()
                take(n, 2 - d, col)

    def strips(a, jobs, fresh):
        if fresh:
            cubed[a] = jnp.zeros((2, 4 * SUBS, BLK), jnp.float32)
            fived[a] = jnp.zeros((6 * SUBS, BLK), jnp.float32)

        def times(left, right):
            return lax.dot_general(
                left, right, (((1,), (1,)), ((), ())), preferred_element_type=jnp.float32
            )

        def one_group(group, carry):
            part = pl.ds(group * APPLY, APPLY)
            c = group // 2
            for step, rows in jobs:
                own = (a + step) * 5
                first, last = place(rows[0]), place(rows[-1]) + 1
                cubed[a, c] = cubed[a, c] + times(
                    pieces[:, (own + first) * LANES : (own + last) * LANES],
                    cubes[a, group, :, (step * 5 + first) * LANES : (step * 5 + last) * LANES],
                )
                if rows != (2,):
                    lanes = slice(step * 2 * LANES, (step + 1) * 2 * LANES)
                    fived[a] = fived[a] + times(
                        moments[a, c, :, lanes], fives[a, group, :, lanes]
                    )
            totals = zeros(APPLY) if fresh else load_acc(a, part)
            for step, rows in jobs:
                for row in rows:
                    for k in range(2):
                        if row not in DISTANT:
                            totals = apply(a, part, row, step, k, totals)
            store_acc(a, part, totals)
            return carry

        lax.fori_loop(0, TILES // APPLY, one_group, 0)

    def finish(n, a):
        value = summed(a, True)
        field[n, a] = value
        vec[n + 1, 2, a + 1] = value * alpha[a]

        @pl.when(n + 1 < SWEEPS)
        def _():
            send(n + 1, a)

    def sweep(n, carry):
        take(n, 2, 1)
        take(n, 2, 2)
        strips(0, [(1, (2,)), (2, (2,))], True)
        strips(1, [(0, (2,)), (1, (2,))], True)
        ready(n, 1)
        strips(0, [(1, OTHERS)], False)
        strips(1, [(0, OTHERS)], False)
        ready(n, 2)
        strips(1, [(1, OTHERS)], False)
        ready(n, 0)
        strips(0, [(2, OTHERS), (0, EVERY)], False)
        finish(n, 0)
        ready(n, 3)
        strips(1, [(2, EVERY)], False)
        finish(n, 1)
        return carry

    lax.fori_loop(0, SWEEPS, sweep, 0)

    lines = []
    for i, j in GRAM:
        product = field[i, 0] * (alpha[0] * field[j, 0]) + field[i, 1] * (alpha[1] * field[j, 1])
        lines.append(jnp.sum(product, axis=0, keepdims=True))
    lines.append(jnp.zeros((16 - len(GRAM), LANES), jnp.float32))
    total = jnp.concatenate(lines, axis=0)
    first = base + SWEEPS * len(HALO)
    for stage, (members, mine) in enumerate(stages):
        gram[stage, mine] = total
        copies = []
        for index, member in enumerate(members):
            copies.append(
                pltpu.make_async_remote_copy(
                    src_ref=gram.at[stage, mine],
                    dst_ref=gram.at[stage, mine],
                    send_sem=send_sem.at[first + index],
                    recv_sem=recv_sem.at[first + index],
                    device_id=member,
                    device_id_type=MESH,
                )
            )
            copies[-1].start()
        for copy in copies:
            copy.wait()
        first += len(members)
        total = gram[stage, 0]
        for index in range(1, len(members) + 1):
            total = total + gram[stage, index]

    sums = jnp.broadcast_to(jnp.sum(total, axis=1, keepdims=True), (16, LANES))
    entry = {}
    for index, (i, j) in enumerate(GRAM):
        entry[i, j] = entry[j, i] = sums[index : index + 1, :]

    def inner(left, right):
        value = None
        for i, u in enumerate(left):
            for j, v in enumerate(right):
                term = u * v * entry[i, j]
                value = term if value is None else value + term
        return value

    one = jnp.ones((1, LANES), jnp.float32)
    residual, direction = [one], [one]
    dipole = []
    rz_value = inner(residual, residual)
    for iteration in range(ITERS):
        size = iteration + 1
        image = [
            (direction[k] if k < size else 0.0) - (direction[k - 1] if k > 0 else 0.0)
            for k in range(size + 1)
        ]
        length = rz_value / inner(direction, image)
        dipole = [
            length * direction[k] + (dipole[k] if k < len(dipole) else 0.0) for k in range(size)
        ]
        residual = [
            (residual[k] if k < size else 0.0) - length * image[k] for k in range(size + 1)
        ]
        if iteration + 1 < ITERS:
            rz_next = inner(residual, residual)
            ratio = rz_next / rz_value
            direction = [
                residual[k] + (ratio * direction[k] if k < size else 0.0) for k in range(size + 1)
            ]
            rz_value = rz_next

    for a in range(2):
        moved = direct[a]
        for k in range(ITERS):
            moved = moved + dipole[k] * field[k, a]
        moved = moved * alpha[a]
        left = residual[0] * field[0, a]
        for k in range(1, ITERS + 1):
            left = left + residual[k] * field[k, a]
        for k in range(3):
            for c in range(2):
                lanes = slice(a * BLK + c * LANES, a * BLK + (c + 1) * LANES)
                dip_ref[k : k + 1, lanes] = moved[2 * k + c : 2 * k + c + 1, :]
                res_ref[k : k + 1, lanes] = left[2 * k + c : 2 * k + c + 1, :]


def on_device(spaces, pairs, span_y, positions, polarizability, charges, groups, pair_list, tile_count):
    atoms = positions.shape[1]
    listed = pair_list.shape[1]
    copies = len(NEAR) + SWEEPS * len(HALO) + 2 * pairs + span_y + spaces // (2 * span_y) - 3
    share = jax.ShapeDtypeStruct((3, 2 * BLK), jnp.float32)
    vmem = pl.BlockSpec(memory_space=pltpu.VMEM)
    hbm = pl.BlockSpec(memory_space=pltpu.HBM)
    return pl.pallas_call(
        functools.partial(kernel, spaces, pairs, span_y),
        out_shape=(share, share),
        in_specs=[hbm] * 5 + [pl.BlockSpec(memory_space=pltpu.SMEM)],
        out_specs=(vmem, vmem),
        scratch_shapes=[
            pltpu.VMEM((3, atoms), jnp.float32),
            pltpu.VMEM((1, atoms), jnp.float32),
            pltpu.VMEM((1, atoms), jnp.float32),
            pltpu.VMEM((1, atoms), jnp.int32),
            pltpu.VMEM((2, listed), jnp.int32),
            pltpu.VMEM((32, LANES), jnp.float32),
            pltpu.VMEM((5, 4, 3, SUBS, LANES), jnp.float32),
            pltpu.VMEM((5, 4, 2, 6, SUBS, LANES), jnp.float32),
            pltpu.VMEM((2, 5, TILES, SUBS, LANES), jnp.float32),
            pltpu.VMEM((30, 3, SUBS, LANES), jnp.float32),
            pltpu.VMEM((60, 3, TILES, SUBS, LANES), jnp.float32),
            pltpu.VMEM((2, 4, BLK, 15 * LANES), jnp.bfloat16),
            pltpu.VMEM((2, 2, 4 * SUBS, BLK), jnp.float32),
            pltpu.VMEM((2, 4, BLK, 6 * LANES), jnp.bfloat16),
            pltpu.VMEM((2, 6 * SUBS, BLK), jnp.float32),
            pltpu.VMEM((2, 3, 2, 2, 3, SUBS, LANES), jnp.float32),
            pltpu.VMEM((2, 2, SUBS, LANES), jnp.float32),
            pltpu.VMEM((2, 2, 6 * SUBS, 6 * LANES), jnp.bfloat16),
            pltpu.VMEM((2, 3, TILES, SUBS, LANES), jnp.float32),
            pltpu.VMEM((2, 8, LANES), jnp.float32),
            pltpu.VMEM((2, 8, LANES), jnp.float32),
            pltpu.VMEM((SWEEPS + 1, 5, 4, SUBS, LANES), jnp.float32),
            pltpu.VMEM((5, 4, 6, SUBS, LANES), jnp.float32),
            pltpu.VMEM((4 * SUBS, 20 * LANES), jnp.bfloat16),
            pltpu.VMEM((SWEEPS, 2, 8, LANES), jnp.float32),
            pltpu.VMEM((3, 8, 16, LANES), jnp.float32),
            pltpu.SemaphoreType.DMA((5,)),
            pltpu.SemaphoreType.DMA((copies,)),
            pltpu.SemaphoreType.DMA((copies,)),
        ],
        compiler_params=pltpu.CompilerParams(
            collective_id=0, has_side_effects=True, vmem_limit_bytes=52 * 2**20
        ),
    )(
        *[
            pltpu.with_memory_space_constraint(value, pltpu.HBM)
            for value in (
                positions,
                polarizability[None],
                charges[None],
                groups[None],
                pair_list[0].T,
            )
        ],
        tile_count,
    )


def solution(mesh):
    spaces, pairs = mesh.shape["space"], mesh.shape["pair"]
    span_y = 8 if spaces >= 128 else 2
    return jax.shard_map(
        functools.partial(on_device, spaces, pairs, span_y),
        mesh=mesh,
        in_specs=(
            P(None, "space"),
            P("space"),
            P("space"),
            P("space"),
            P("space", None, None),
            P("space"),
        ),
        out_specs=(P(None, ("space", "pair")), P(None, ("space", "pair"))),
        check_vma=False,
    )
```

```python
import functools

import jax
import jax.numpy as jnp
from jax import lax
from jax.experimental import pallas as pl
from jax.experimental.pallas import tpu as pltpu
from jax.sharding import PartitionSpec as P

BLK = 256
BPD = 8
ITERS = 3
LANES = 128
SUBS = 8
TILES = BLK // SUBS
BUILD = 4
APPLY = 8
PERIOD = BPD * 8 * 2.15
THOLE = 0.39
ROOT_THREE = 3.0**0.5
SWEEPS = ITERS + 1
MESH = pl.DeviceIdType.MESH

NEAR = [-2, -1, 1, 2]
SEAT = {1: 0, 2: 1, 0: 2, 3: 3}
COPIES = 2 + 2 * len(NEAR)
X, Y, Z, GROUP, ROOT, CHARGE = range(6)
OTHERS = (0, 1, 3, 4)
EVERY = OTHERS + (2,)
DISTANT = (0, 4)
GRAM = [(i, j) for i in range(ITERS) for j in range(i, ITERS + 1)]


def kernel(
    spaces,
    pairs,
    span_y,
    positions_ref,
    polar_ref,
    charges_ref,
    groups_ref,
    list_ref,
    count_ref,
    dip_ref,
    res_ref,
    positions,
    polar,
    charges,
    groups,
    listing,
    flags,
    window,
    wide,
    column,
    weight,
    coef,
    cubes,
    cubed,
    fives,
    fived,
    apart,
    centred,
    moments,
    acc,
    alpha,
    direct,
    vec,
    spread,
    pieces,
    field,
    gram,
    load_sem,
    send_sem,
    recv_sem,
):
    loads = [
        pltpu.make_async_copy(source, target, load_sem.at[index])
        for index, (source, target) in enumerate(
            (
                (positions_ref, positions),
                (polar_ref, polar),
                (charges_ref, charges),
                (groups_ref, groups),
                (list_ref, listing),
            )
        )
    ]
    for load in loads:
        load.start()

    sp = lax.axis_index("space")
    pr = lax.axis_index("pair")
    core = lax.rem(sp, 2)
    y = lax.rem(sp // 2, span_y)
    z = sp // (2 * span_y)
    span_z = spaces // (2 * span_y)

    def at_space(d):
        return lax.rem(sp + (d + spaces), spaces)

    def at_pair(e):
        return lax.rem(pr + (e + pairs), pairs)

    def at_core(c):
        return sp - core + lax.rem(core + c, 2)

    stages = [
        (
            [(at_core(c), at_pair(k)) for k in range(pairs) for c in range(2) if (k, c) != (0, 0)],
            pr * 2 + core,
        ),
        (
            [(sp + (lax.rem(y + k, span_y) - y) * 2, pr) for k in range(1, span_y)],
            y,
        ),
        (
            [(sp + (lax.rem(z + k, span_z) - z) * 2 * span_y, pr) for k in range(1, span_z)],
            z,
        ),
    ]

    barrier = pltpu.get_barrier_semaphore()
    partners = [(at_space(d), pr) for d in NEAR]
    for members, _ in stages:
        partners = partners + members
    for partner in partners:
        pl.semaphore_signal(barrier, inc=1, device_id=partner, device_id_type=MESH)

    for load in loads:
        load.wait()

    slot, partner = listing[0:1, :], listing[1:2, :]
    row_step = partner // BPD - sp
    col_step = (partner % BPD - slot + (BPD + 1)) % BPD - 1
    kind = jnp.where(row_step == 0, col_step, row_step * 3 + col_step)
    entry = lax.broadcasted_iota(jnp.int32, slot.shape, 1)
    key = jnp.where(entry < count_ref[0], kind * BPD + slot, -1)
    wanted = lax.broadcasted_iota(jnp.int32, (32, slot.shape[1]), 0)
    wanted = (wanted // 4) * BPD + (2 * pr + (BPD - 1) + wanted % 4) % BPD
    found = jnp.max((key == wanted).astype(jnp.float32), axis=1, keepdims=True)
    flags[...] = jnp.broadcast_to(found, (32, LANES))

    low = jnp.where(pr == 0, -PERIOD, 0.0).astype(jnp.float32)
    high = jnp.where(pr == pairs - 1, PERIOD, 0.0).astype(jnp.float32)
    for k in range(4):
        block = lax.rem(2 * pr + (k - 1 + BPD), BPD)
        for c in range(2):
            lanes = pl.ds(pl.multiple_of(block * BLK + c * LANES, LANES), LANES)
            shift = {0: low, 3: high}.get(k, 0.0)
            lines = {
                X: positions[0:1, lanes] + shift,
                Y: positions[1:2, lanes],
                Z: positions[2:3, lanes],
                GROUP: groups[0:1, lanes].astype(jnp.float32),
                ROOT: lax.rsqrt(polar[0:1, lanes]),
                CHARGE: charges[0:1, lanes],
            }
            for line, value in lines.items():
                window[2, k, c, line : line + 1, :] = value
            window[2, k, c, 6:8, :] = jnp.zeros((2, LANES), jnp.float32)
            if k in (1, 2):
                for m in range(3):
                    alpha[k - 1, 2 * m + c : 2 * m + c + 1, :] = polar[0:1, lanes]
        for m in range(8):
            window[2, k, 2, m : m + 1, :] = flags[4 * m + k : 4 * m + k + 1, :]

    def place(row):
        return EVERY.index(row)

    def widen(row, col):
        for c in range(2):
            for k in range(6):
                line = window[row, col, c, k : k + 1, :]
                wide[row, col, c, k] = jnp.broadcast_to(line, (SUBS, LANES))

    def widen_own(col, carry):
        widen(2, col)
        return carry

    def widen_rest(index, carry):
        row = index // 4
        widen(row + row // 2, index % 4)
        return carry

    pl.semaphore_wait(barrier, len(partners))

    def attr_copy(index, d):
        return pltpu.make_async_remote_copy(
            src_ref=window.at[2],
            dst_ref=window.at[2 - d],
            send_sem=send_sem.at[index],
            recv_sem=recv_sem.at[index],
            device_id=(at_space(d), pr),
            device_id_type=MESH,
        )

    for index, d in enumerate(NEAR):
        attr_copy(index, d).start()

    for a in range(2):
        for c in range(2):
            turned = window[2, a + 1, c].T
            for k in (X, Y, Z, GROUP, ROOT):
                values = jnp.broadcast_to(turned[:, k : k + 1], (LANES, LANES))
                if k == ROOT:
                    values = values * -THOLE
                half = LANES // SUBS
                column[a, k, c * half : (c + 1) * half] = values.reshape(half, SUBS, LANES)
        alpha[a, 6:8, :] = jnp.zeros((2, LANES), jnp.float32)

    sublane = lax.broadcasted_iota(jnp.int32, (SUBS, LANES), 0)
    fourth = lax.rem(sublane, 4)

    def choose(x, y, z, other):
        return jnp.where(
            fourth == 0, x, jnp.where(fourth == 1, y, jnp.where(fourth == 2, z, other))
        )

    def centre(a):
        mean = jnp.sum(window[2, a + 1, 0] + window[2, a + 1, 1], axis=1, keepdims=True) / BLK
        return [jnp.broadcast_to(mean[k : k + 1, :], (SUBS, LANES)) for k in range(3)]

    def set_apart():
        for a in range(2):
            middle = centre(a)
            for step in range(3):
                for index, row in enumerate(DISTANT):
                    for c in range(2):
                        for k in range(3):
                            apart[a, step, index, c, k] = wide[row, a + step, c, k] - middle[k]
            for c in range(2):
                own = [wide[2, a + 1, c, k] - middle[k] for k in range(3)]
                centred[a, c] = choose(*own, -1.0)

    def weigh(a, row, step):
        slot = a * 15 + row * 3 + step
        dx = step - 1
        if row == 2:
            entry, col = (abs(dx), a + step if dx < 0 else a + 1)
        elif row > 2:
            entry, col = ((2, 5)[row - 3] + dx + 1, a + 1)
        else:
            entry, col = ((5, 2)[row] - dx + 1, a + step)
        line = window[min(row, 2), col, 2, entry : entry + 1, :]
        weight[slot, 0] = jnp.broadcast_to(line, (SUBS, LANES))
        weight[slot, 1] = jnp.broadcast_to(line * ROOT_THREE, (SUBS, LANES))
        weight[slot, 2] = jnp.broadcast_to(line * 3.0, (SUBS, LANES))

    def build(a, part, row, step, c, totals, itself, masked):
        def far(line):
            return wide[row, a + step, c, line]

        rx = column[a, X, part] - far(X)
        ry = column[a, Y, part] - far(Y)
        rz = column[a, Z, part] - far(Z)
        squared = rx * rx + ry * ry + rz * rz
        if itself:
            squared = jnp.maximum(squared, 1.0)
        inverse = lax.rsqrt(squared)
        inverse_sq = inverse * inverse
        damping = (squared * (squared * inverse)) * (column[a, ROOT, part] * far(ROOT))
        decayed = jnp.exp(damping)
        third = 1.0 - decayed
        fifth = (third + damping * decayed) * inverse
        tile = a * 15 + row * 3 + step
        three = (third * (inverse_sq * inverse)) * weight[tile, 0]
        rows = pl.ds(pl.multiple_of(part.start * SUBS, BUILD * SUBS), BUILD * SUBS)

        def keep(matrices, value, lanes):
            flat = value.reshape(BUILD * SUBS, LANES)
            high = flat.astype(jnp.bfloat16)
            low = (flat - high.astype(jnp.float32)).astype(jnp.bfloat16)
            matrices[a, 2 * c, rows, lanes] = high
            matrices[a, 2 * c + 1, rows, lanes] = low

        if row in DISTANT:
            five = (fifth * (inverse_sq * inverse_sq)) * weight[tile, 2]
            lane = (step * 2 + DISTANT.index(row)) * LANES
            keep(fives, five, slice(lane, lane + LANES))
        else:
            root = (fifth * lax.rsqrt(fifth)) * (inverse_sq * weight[tile, 1])
            index = tile * 2 + c
            coef[index, 0, part] = rx * root
            coef[index, 1, part] = ry * root
            coef[index, 2, part] = rz * root
        if itself:
            shape = (BUILD, SUBS, LANES)
            own = lax.broadcasted_iota(jnp.int32, shape, 0) * SUBS + part.start * SUBS
            own = own + lax.broadcasted_iota(jnp.int32, shape, 1)
            other = lax.broadcasted_iota(jnp.int32, shape, 2) + c * LANES
            three = jnp.where(own == other, 0.0, three)
        lane = (step * 5 + place(row)) * LANES
        keep(cubes, three, slice(lane, lane + LANES))
        charged = three * far(CHARGE)
        if masked:
            charged = jnp.where(column[a, GROUP, part] != far(GROUP), charged, 0.0)
        ex, ey, ez = totals
        return (ex + charged * rx, ey + charged * ry, ez + charged * rz)

    def apply(a, part, row, step, c, totals):
        index = (a * 15 + row * 3 + step) * 2 + c
        sx, sy, sz = (coef[index, k, part] for k in range(3))
        vx, vy, vz = (spread[row, a + step, 2 * k + c] for k in range(3))
        along = sx * vx + sy * vy + sz * vz
        ex, ey, ez = totals
        return (ex + along * sx, ey + along * sy, ez + along * sz)

    def zeros(size):
        return tuple(jnp.zeros((size, SUBS, LANES), jnp.float32) for _ in range(3))

    def load_acc(a, part):
        return tuple(acc[a, k, part] for k in range(3))

    def store_acc(a, part, totals):
        for k in range(3):
            acc[a, k, part] = totals[k]

    def summed(a, with_cubes):
        if with_cubes:
            less = [
                cubed[a, c, 0:8] + cubed[a, c, 8:16] + cubed[a, c, 16:24] for c in range(2)
            ]
            expanded = []
            for c in range(2):
                lanes = slice(c * LANES, (c + 1) * LANES)
                sums = []
                for half in range(2):
                    first = half * SUBS
                    piece = [fived[a, first + 16 * m : first + 16 * m + 8, lanes] for m in range(3)]
                    terms = (piece[0] + piece[1] + piece[2]) * centred[a, c]
                    for quarter in range(2):
                        rows = terms[4 * quarter : 4 * quarter + 4, :]
                        sums.append(jnp.sum(rows, axis=0, keepdims=True))
                expanded.append(sums)
        parts = []
        for k in range(3):
            for c in range(2):
                half = LANES // SUBS
                turned = acc[a, k, c * half : (c + 1) * half].reshape(LANES, LANES).T
                part = jnp.sum(turned, axis=0, keepdims=True)
                if with_cubes:
                    lanes = slice(c * LANES, (c + 1) * LANES)
                    part = part - (
                        less[0][2 * k : 2 * k + 1, lanes] + less[1][2 * k + 1 : 2 * k + 2, lanes]
                    )
                    own = centred[a, c][k : k + 1, :]
                    part = part + (own * expanded[c][0] - expanded[c][k + 1])
                parts.append(part)
        parts.append(jnp.zeros((2, LANES), jnp.float32))
        return jnp.concatenate(parts, axis=0)

    base = len(NEAR)

    def remote(source, target, number, device):
        return pltpu.make_async_remote_copy(
            src_ref=source,
            dst_ref=target,
            send_sem=send_sem.at[number],
            recv_sem=recv_sem.at[number],
            device_id=device,
            device_id_type=MESH,
        )

    def beside(n, block):
        target = vec.at[n, 2, SEAT[0 if block else 3]]
        device = (sp, at_pair(1 if block else -1))
        return remote(vec.at[n, 2, block], target, base + n * COPIES + block, device)

    def across(n, half):
        seats = pl.ds(2 * half, 2)
        return [
            remote(
                vec.at[n, 2, seats],
                vec.at[n, 2 - d, seats],
                base + n * COPIES + 2 + half * len(NEAR) + index,
                (at_space(d), pr),
            )
            for index, d in enumerate(NEAR)
        ]

    def send(n, block):
        beside(n, block).start()
        if block == 1:
            for copy in across(n, 0):
                copy.start()

    for a in range(2):
        for step in range(3):
            for row in (2, 3, 4):
                weigh(a, row, step)

    lax.fori_loop(0, 4, widen_own, 0)

    def build_own(group, carry):
        a = group // (TILES // BUILD)
        part = pl.ds((group - a * (TILES // BUILD)) * BUILD, BUILD)
        totals = zeros(BUILD)
        for step in range(3):
            for c in range(2):
                totals = build(a, part, 2, step, c, totals, step == 1, True)
        store_acc(a, part, totals)
        return carry

    lax.fori_loop(0, 2 * (TILES // BUILD), build_own, 0)
    for index, d in enumerate(NEAR):
        attr_copy(index, d).wait()
    for a in range(2):
        for step in range(3):
            for row in (0, 1):
                weigh(a, row, step)
    lax.fori_loop(0, 16, widen_rest, 0)
    set_apart()

    def build_rest(a, carry):
        def one_group(group, inner):
            part = pl.ds(group * BUILD, BUILD)

            totals = load_acc(a, part)
            for row in OTHERS:
                for step in range(3):
                    for c in range(2):
                        masked = (row, step) in ((1, 0), (3, 2))
                        totals = build(a, part, row, step, c, totals, False, masked)
            store_acc(a, part, totals)
            return inner

        lax.fori_loop(0, TILES // BUILD, one_group, 0)
        value = summed(a, False)
        direct[a] = value
        vec[0, 2, a] = value * alpha[a]
        for block in range(2):

            @pl.when(a == block)
            def _():
                send(0, block)

        return carry

    lax.fori_loop(0, 2, build_rest, 0)

    def thirds(value):
        high = value.astype(jnp.bfloat16).astype(jnp.float32)
        rest = value - high
        middle = rest.astype(jnp.bfloat16).astype(jnp.float32)
        return [high, middle, rest - middle]

    def take(n, row, col):
        tile = vec[n, row, SEAT[col]]
        lines = [jnp.broadcast_to(tile[m : m + 1, :], (SUBS, LANES)) for m in range(6)]
        parts = jnp.concatenate(thirds(tile) + [jnp.zeros_like(tile)], axis=0)
        lane = (col * 5 + place(row)) * LANES
        pieces[:, lane : lane + LANES] = parts.astype(jnp.bfloat16)
        if row not in DISTANT:
            for m in range(6):
                spread[row, col, m] = lines[m]
            return
        index = DISTANT.index(row)
        for a in range(2):
            step = col - a
            if not 0 <= step < 3:
                continue
            for c in range(2):
                x, y, z = (apart[a, step, index, c, k] for k in range(3))
                vx, vy, vz = (lines[2 * k + c] for k in range(3))
                four = choose(vx, vy, vz, x * vx + y * vy + z * vz)
                upper = four * jnp.where(sublane < 4, 1.0, x)
                lower = four * jnp.where(sublane < 4, y, z)
                uppers, lowers = thirds(upper), thirds(lower)
                parts = [value for pair in zip(uppers, lowers) for value in pair]
                lane = (step * 2 + index) * LANES
                moments[a, c, :, lane : lane + LANES] = jnp.concatenate(parts, axis=0).astype(
                    jnp.bfloat16
                )

    def strips(a, jobs, fresh):
        if fresh:
            cubed[a] = jnp.zeros((2, 4 * SUBS, BLK), jnp.float32)
            fived[a] = jnp.zeros((6 * SUBS, BLK), jnp.float32)

        def times(left, right):
            return lax.dot_general(
                left, right, (((1,), (1,)), ((), ())), preferred_element_type=jnp.float32
            )

        def one_group(group, carry):
            part = pl.ds(group * APPLY, APPLY)
            c = group // 2
            for step, rows in jobs:
                own = (a + step) * 5
                first, last = place(rows[0]), place(rows[-1]) + 1
                cubed[a, c] = cubed[a, c] + times(
                    pieces[:, (own + first) * LANES : (own + last) * LANES],
                    cubes[a, group, :, (step * 5 + first) * LANES : (step * 5 + last) * LANES],
                )
                if rows != (2,):
                    lanes = slice(step * 2 * LANES, (step + 1) * 2 * LANES)
                    fived[a] = fived[a] + times(
                        moments[a, c, :, lanes], fives[a, group, :, lanes]
                    )
            totals = zeros(APPLY) if fresh else load_acc(a, part)
            for step, rows in jobs:
                for row in rows:
                    for k in range(2):
                        if row not in DISTANT:
                            totals = apply(a, part, row, step, k, totals)
            store_acc(a, part, totals)
            return carry

        lax.fori_loop(0, TILES // APPLY, one_group, 0)

    def finish(n, a):
        value = summed(a, True)
        field[n, a] = value
        vec[n + 1, 2, a] = value * alpha[a]

        @pl.when(n + 1 < SWEEPS)
        def _():
            send(n + 1, a)

    def sweep(n, carry):
        take(n, 2, 1)
        take(n, 2, 2)
        strips(0, [(1, (2,)), (2, (2,))], True)
        strips(1, [(0, (2,)), (1, (2,))], True)
        for block in range(2):
            beside(n, block).wait_recv()
        for copy in across(n, 1):
            copy.start()
        take(n, 2, 0)
        take(n, 2, 3)
        for index, copy in enumerate(across(n, 0)):
            copy.wait_recv()
            for col in (1, 2):
                take(n, 2 - NEAR[index], col)
        strips(0, [(1, OTHERS), (2, OTHERS), (0, (2,))], False)
        strips(1, [(0, OTHERS), (1, OTHERS), (2, (2,))], False)
        for index, copy in enumerate(across(n, 1)):
            copy.wait_recv()
            for col in (0, 3):
                take(n, 2 - NEAR[index], col)
        strips(0, [(0, OTHERS)], False)
        finish(n, 0)
        strips(1, [(2, OTHERS)], False)
        finish(n, 1)
        return carry

    lax.fori_loop(0, SWEEPS, sweep, 0)

    lines = []
    for i, j in GRAM:
        product = field[i, 0] * (alpha[0] * field[j, 0]) + field[i, 1] * (alpha[1] * field[j, 1])
        lines.append(jnp.sum(product, axis=0, keepdims=True))
    lines.append(jnp.zeros((16 - len(GRAM), LANES), jnp.float32))
    total = jnp.concatenate(lines, axis=0)
    first = base + SWEEPS * COPIES
    pending = []
    for stage, (members, mine) in enumerate(stages):
        gram[stage, mine] = total
        copies = [
            remote(gram.at[stage, mine], gram.at[stage, mine], first + index, member)
            for index, member in enumerate(members)
        ]
        for copy in copies:
            copy.start()
        if stage == 0:

            def sent(n, carry):
                for copy in [beside(n, 0), beside(n, 1)] + across(n, 0) + across(n, 1):
                    copy.wait_send()
                return carry

            lax.fori_loop(0, SWEEPS, sent, 0)
        for copy in pending:
            copy.wait_send()
        pending = copies
        for copy in copies:
            copy.wait_recv()
        first += len(members)
        total = gram[stage, 0]
        for index in range(1, len(members) + 1):
            total = total + gram[stage, index]

    sums = jnp.broadcast_to(jnp.sum(total, axis=1, keepdims=True), (16, LANES))
    entry = {}
    for index, (i, j) in enumerate(GRAM):
        entry[i, j] = entry[j, i] = sums[index : index + 1, :]

    def inner(left, right):
        value = None
        for i, u in enumerate(left):
            for j, v in enumerate(right):
                term = u * v * entry[i, j]
                value = term if value is None else value + term
        return value

    one = jnp.ones((1, LANES), jnp.float32)
    residual, direction = [one], [one]
    dipole = []
    rz_value = inner(residual, residual)
    for iteration in range(ITERS):
        size = iteration + 1
        image = [
            (direction[k] if k < size else 0.0) - (direction[k - 1] if k > 0 else 0.0)
            for k in range(size + 1)
        ]
        length = rz_value / inner(direction, image)
        dipole = [
            length * direction[k] + (dipole[k] if k < len(dipole) else 0.0) for k in range(size)
        ]
        residual = [
            (residual[k] if k < size else 0.0) - length * image[k] for k in range(size + 1)
        ]
        if iteration + 1 < ITERS:
            rz_next = inner(residual, residual)
            ratio = rz_next / rz_value
            direction = [
                residual[k] + (ratio * direction[k] if k < size else 0.0) for k in range(size + 1)
            ]
            rz_value = rz_next

    for a in range(2):
        moved = direct[a]
        for k in range(ITERS):
            moved = moved + dipole[k] * field[k, a]
        moved = moved * alpha[a]
        left = residual[0] * field[0, a]
        for k in range(1, ITERS + 1):
            left = left + residual[k] * field[k, a]
        for k in range(3):
            for c in range(2):
                lanes = slice(a * BLK + c * LANES, a * BLK + (c + 1) * LANES)
                dip_ref[k : k + 1, lanes] = moved[2 * k + c : 2 * k + c + 1, :]
                res_ref[k : k + 1, lanes] = left[2 * k + c : 2 * k + c + 1, :]
    for copy in pending:
        copy.wait_send()


def on_device(spaces, pairs, span_y, positions, polarizability, charges, groups, pair_list, tile_count):
    atoms = positions.shape[1]
    listed = pair_list.shape[1]
    copies = len(NEAR) + SWEEPS * COPIES + 2 * pairs + span_y + spaces // (2 * span_y) - 3
    share = jax.ShapeDtypeStruct((3, 2 * BLK), jnp.float32)
    vmem = pl.BlockSpec(memory_space=pltpu.VMEM)
    hbm = pl.BlockSpec(memory_space=pltpu.HBM)
    return pl.pallas_call(
        functools.partial(kernel, spaces, pairs, span_y),
        out_shape=(share, share),
        in_specs=[hbm] * 5 + [pl.BlockSpec(memory_space=pltpu.SMEM)],
        out_specs=(vmem, vmem),
        scratch_shapes=[
            pltpu.VMEM((3, atoms), jnp.float32),
            pltpu.VMEM((1, atoms), jnp.float32),
            pltpu.VMEM((1, atoms), jnp.float32),
            pltpu.VMEM((1, atoms), jnp.int32),
            pltpu.VMEM((2, listed), jnp.int32),
            pltpu.VMEM((32, LANES), jnp.float32),
            pltpu.VMEM((5, 4, 3, SUBS, LANES), jnp.float32),
            pltpu.VMEM((5, 4, 2, 6, SUBS, LANES), jnp.float32),
            pltpu.VMEM((2, 5, TILES, SUBS, LANES), jnp.float32),
            pltpu.VMEM((30, 3, SUBS, LANES), jnp.float32),
            pltpu.VMEM((60, 3, TILES, SUBS, LANES), jnp.float32),
            pltpu.VMEM((2, 4, BLK, 15 * LANES), jnp.bfloat16),
            pltpu.VMEM((2, 2, 4 * SUBS, BLK), jnp.float32),
            pltpu.VMEM((2, 4, BLK, 6 * LANES), jnp.bfloat16),
            pltpu.VMEM((2, 6 * SUBS, BLK), jnp.float32),
            pltpu.VMEM((2, 3, 2, 2, 3, SUBS, LANES), jnp.float32),
            pltpu.VMEM((2, 2, SUBS, LANES), jnp.float32),
            pltpu.VMEM((2, 2, 6 * SUBS, 6 * LANES), jnp.bfloat16),
            pltpu.VMEM((2, 3, TILES, SUBS, LANES), jnp.float32),
            pltpu.VMEM((2, 8, LANES), jnp.float32),
            pltpu.VMEM((2, 8, LANES), jnp.float32),
            pltpu.VMEM((SWEEPS + 1, 5, 4, SUBS, LANES), jnp.float32),
            pltpu.VMEM((5, 4, 6, SUBS, LANES), jnp.float32),
            pltpu.VMEM((4 * SUBS, 20 * LANES), jnp.bfloat16),
            pltpu.VMEM((SWEEPS, 2, 8, LANES), jnp.float32),
            pltpu.VMEM((3, 8, 16, LANES), jnp.float32),
            pltpu.SemaphoreType.DMA((5,)),
            pltpu.SemaphoreType.DMA((copies,)),
            pltpu.SemaphoreType.DMA((copies,)),
        ],
        compiler_params=pltpu.CompilerParams(
            collective_id=0, has_side_effects=True, vmem_limit_bytes=52 * 2**20
        ),
    )(
        *[
            pltpu.with_memory_space_constraint(value, pltpu.HBM)
            for value in (
                positions,
                polarizability[None],
                charges[None],
                groups[None],
                pair_list[0].T,
            )
        ],
        tile_count,
    )


def solution(mesh):
    spaces, pairs = mesh.shape["space"], mesh.shape["pair"]
    span_y = 8 if spaces >= 128 else 2
    return jax.shard_map(
        functools.partial(on_device, spaces, pairs, span_y),
        mesh=mesh,
        in_specs=(
            P(None, "space"),
            P("space"),
            P("space"),
            P("space"),
            P("space", None, None),
            P("space"),
        ),
        out_specs=(P(None, ("space", "pair")), P(None, ("space", "pair"))),
        check_vma=False,
    )
```

```python
import functools

import jax
import jax.numpy as jnp
from jax import lax
from jax.experimental import pallas as pl
from jax.experimental.pallas import tpu as pltpu
from jax.sharding import PartitionSpec as P

BLK = 256
BPD = 8
ITERS = 3
LANES = 128
SUBS = 8
TILES = BLK // SUBS
BUILD = 4
APPLY = 8
PERIOD = BPD * 8 * 2.15
THOLE = 0.39
ROOT_THREE = 3.0**0.5
SWEEPS = ITERS + 1
MESH = pl.DeviceIdType.MESH

NEAR = [-2, -1, 1, 2]
REACH = [-2, 2, -1, 1, 0]
TARGETS = {1: (0, 0, NEAR), 3: (0, -1, REACH), 2: (1, 0, NEAR), 0: (1, 1, REACH)}
HALO = [(column, d) for column in (1, 3, 2, 0) for d in TARGETS[column][2]]
X, Y, Z, GROUP, ROOT, CHARGE = range(6)
OTHERS = (0, 1, 3, 4)
EVERY = OTHERS + (2,)
GRAM = [(i, j) for i in range(ITERS) for j in range(i, ITERS + 1)]


def kernel(
    spaces,
    pairs,
    span_y,
    positions_ref,
    polar_ref,
    charges_ref,
    groups_ref,
    list_ref,
    count_ref,
    dip_ref,
    res_ref,
    positions,
    polar,
    charges,
    groups,
    listing,
    flags,
    window,
    wide,
    column,
    weight,
    coef,
    cubes,
    cubed,
    acc,
    alpha,
    direct,
    vec,
    spread,
    pieces,
    field,
    gram,
    load_sem,
    send_sem,
    recv_sem,
):
    loads = [
        pltpu.make_async_copy(source, target, load_sem.at[index])
        for index, (source, target) in enumerate(
            (
                (positions_ref, positions),
                (polar_ref, polar),
                (charges_ref, charges),
                (groups_ref, groups),
                (list_ref, listing),
            )
        )
    ]
    for load in loads:
        load.start()

    sp = lax.axis_index("space")
    pr = lax.axis_index("pair")
    core = lax.rem(sp, 2)
    y = lax.rem(sp // 2, span_y)
    z = sp // (2 * span_y)
    span_z = spaces // (2 * span_y)

    def at_space(d):
        return lax.rem(sp + (d + spaces), spaces)

    def at_pair(e):
        return lax.rem(pr + (e + pairs), pairs)

    def at_core(c):
        return sp - core + lax.rem(core + c, 2)

    stages = [
        (
            [(at_core(c), at_pair(k)) for k in range(pairs) for c in range(2) if (k, c) != (0, 0)],
            pr * 2 + core,
        ),
        (
            [(sp + (lax.rem(y + k, span_y) - y) * 2, pr) for k in range(1, span_y)],
            y,
        ),
        (
            [(sp + (lax.rem(z + k, span_z) - z) * 2 * span_y, pr) for k in range(1, span_z)],
            z,
        ),
    ]

    barrier = pltpu.get_barrier_semaphore()
    partners = [(at_space(d), at_pair(e)) for d in REACH for e in (-1, 0, 1) if (d, e) != (0, 0)]
    for members, _ in stages:
        partners = partners + members
    for partner in partners:
        pl.semaphore_signal(barrier, inc=1, device_id=partner, device_id_type=MESH)

    for load in loads:
        load.wait()

    slot, partner = listing[0:1, :], listing[1:2, :]
    row_step = partner // BPD - sp
    col_step = (partner % BPD - slot + (BPD + 1)) % BPD - 1
    kind = jnp.where(row_step == 0, col_step, row_step * 3 + col_step)
    entry = lax.broadcasted_iota(jnp.int32, slot.shape, 1)
    key = jnp.where(entry < count_ref[0], kind * BPD + slot, -1)
    wanted = lax.broadcasted_iota(jnp.int32, (32, slot.shape[1]), 0)
    wanted = (wanted // 4) * BPD + (2 * pr + (BPD - 1) + wanted % 4) % BPD
    found = jnp.max((key == wanted).astype(jnp.float32), axis=1, keepdims=True)
    flags[...] = jnp.broadcast_to(found, (32, LANES))

    low = jnp.where(pr == 0, -PERIOD, 0.0).astype(jnp.float32)
    high = jnp.where(pr == pairs - 1, PERIOD, 0.0).astype(jnp.float32)
    for k in range(4):
        block = lax.rem(2 * pr + (k - 1 + BPD), BPD)
        for c in range(2):
            lanes = pl.ds(pl.multiple_of(block * BLK + c * LANES, LANES), LANES)
            shift = {0: low, 3: high}.get(k, 0.0)
            lines = {
                X: positions[0:1, lanes] + shift,
                Y: positions[1:2, lanes],
                Z: positions[2:3, lanes],
                GROUP: groups[0:1, lanes].astype(jnp.float32),
                ROOT: lax.rsqrt(polar[0:1, lanes]),
                CHARGE: charges[0:1, lanes],
            }
            for line, value in lines.items():
                window[2, k, c, line : line + 1, :] = value
            window[2, k, c, 6:8, :] = jnp.zeros((2, LANES), jnp.float32)
            if k in (1, 2):
                for m in range(3):
                    alpha[k - 1, 2 * m + c : 2 * m + c + 1, :] = polar[0:1, lanes]
        for m in range(8):
            window[2, k, 2, m : m + 1, :] = flags[4 * m + k : 4 * m + k + 1, :]

    def place(row):
        return EVERY.index(row)

    def widen(row, col):
        for c in range(2):
            for k in range(6):
                line = window[row, col, c, k : k + 1, :]
                wide[row, col, c, k] = jnp.broadcast_to(line, (SUBS, LANES))

    def widen_own(col, carry):
        widen(2, col)
        return carry

    def widen_rest(index, carry):
        row = index // 4
        widen(row + row // 2, index % 4)
        return carry

    pl.semaphore_wait(barrier, len(partners))

    def attr_copy(index, d):
        return pltpu.make_async_remote_copy(
            src_ref=window.at[2],
            dst_ref=window.at[2 - d],
            send_sem=send_sem.at[index],
            recv_sem=recv_sem.at[index],
            device_id=(at_space(d), pr),
            device_id_type=MESH,
        )

    for index, d in enumerate(NEAR):
        attr_copy(index, d).start()

    for a in range(2):
        for c in range(2):
            turned = window[2, a + 1, c].T
            for k in (X, Y, Z, GROUP, ROOT):
                values = jnp.broadcast_to(turned[:, k : k + 1], (LANES, LANES))
                if k == ROOT:
                    values = values * -THOLE
                half = LANES // SUBS
                column[a, k, c * half : (c + 1) * half] = values.reshape(half, SUBS, LANES)
        alpha[a, 6:8, :] = jnp.zeros((2, LANES), jnp.float32)

    def weigh(a, row, step):
        slot = a * 15 + row * 3 + step
        dx = step - 1
        if row == 2:
            entry, col = (abs(dx), a + step if dx < 0 else a + 1)
        elif row > 2:
            entry, col = ((2, 5)[row - 3] + dx + 1, a + 1)
        else:
            entry, col = ((5, 2)[row] - dx + 1, a + step)
        line = window[min(row, 2), col, 2, entry : entry + 1, :]
        weight[slot, 0] = jnp.broadcast_to(line, (SUBS, LANES))
        weight[slot, 1] = jnp.broadcast_to(line * ROOT_THREE, (SUBS, LANES))

    def build(a, part, row, step, c, totals, itself, masked):
        def far(line):
            return wide[row, a + step, c, line]

        rx = column[a, X, part] - far(X)
        ry = column[a, Y, part] - far(Y)
        rz = column[a, Z, part] - far(Z)
        squared = rx * rx + ry * ry + rz * rz
        if itself:
            squared = jnp.maximum(squared, 1.0)
        inverse = lax.rsqrt(squared)
        inverse_sq = inverse * inverse
        damping = (squared * (squared * inverse)) * (column[a, ROOT, part] * far(ROOT))
        decayed = jnp.exp(damping)
        third = 1.0 - decayed
        fifth = (third + damping * decayed) * inverse
        tile = a * 15 + row * 3 + step
        three = (third * (inverse_sq * inverse)) * weight[tile, 0]
        root = (fifth * lax.rsqrt(fifth)) * (inverse_sq * weight[tile, 1])
        index = tile * 2 + c
        coef[index, 0, part] = rx * root
        coef[index, 1, part] = ry * root
        coef[index, 2, part] = rz * root
        if itself:
            shape = (BUILD, SUBS, LANES)
            own = lax.broadcasted_iota(jnp.int32, shape, 0) * SUBS + part.start * SUBS
            own = own + lax.broadcasted_iota(jnp.int32, shape, 1)
            other = lax.broadcasted_iota(jnp.int32, shape, 2) + c * LANES
            three = jnp.where(own == other, 0.0, three)
        flat = three.reshape(BUILD * SUBS, LANES)
        high = flat.astype(jnp.bfloat16)
        low = (flat - high.astype(jnp.float32)).astype(jnp.bfloat16)
        first = pl.multiple_of(part.start * SUBS, BUILD * SUBS)
        rows = pl.ds(first, BUILD * SUBS)
        lanes = pl.ds(pl.multiple_of((step * 5 + place(row)) * LANES, LANES), LANES)
        cubes[a, 2 * c, rows, lanes] = high
        cubes[a, 2 * c + 1, rows, lanes] = low
        charged = three * far(CHARGE)
        if masked:
            charged = jnp.where(column[a, GROUP, part] != far(GROUP), charged, 0.0)
        ex, ey, ez = totals
        return (ex + charged * rx, ey + charged * ry, ez + charged * rz)

    def apply(a, part, row, step, c, totals):
        index = (a * 15 + row * 3 + step) * 2 + c
        sx, sy, sz = (coef[index, k, part] for k in range(3))
        vx, vy, vz = (spread[row, a + step, 2 * k + c] for k in range(3))
        along = sx * vx + sy * vy + sz * vz
        ex, ey, ez = totals
        return (ex + along * sx, ey + along * sy, ez + along * sz)

    def zeros(size):
        return tuple(jnp.zeros((size, SUBS, LANES), jnp.float32) for _ in range(3))

    def load_acc(a, part):
        return tuple(acc[a, k, part] for k in range(3))

    def store_acc(a, part, totals):
        for k in range(3):
            acc[a, k, part] = totals[k]

    def summed(a, with_cubes):
        if with_cubes:
            less = [
                cubed[a, c, 0:8] + cubed[a, c, 8:16] + cubed[a, c, 16:24] for c in range(2)
            ]
        parts = []
        for k in range(3):
            for c in range(2):
                half = LANES // SUBS
                turned = acc[a, k, c * half : (c + 1) * half].reshape(LANES, LANES).T
                part = jnp.sum(turned, axis=0, keepdims=True)
                if with_cubes:
                    lanes = slice(c * LANES, (c + 1) * LANES)
                    part = part - (
                        less[0][2 * k : 2 * k + 1, lanes] + less[1][2 * k + 1 : 2 * k + 2, lanes]
                    )
                parts.append(part)
        parts.append(jnp.zeros((2, LANES), jnp.float32))
        return jnp.concatenate(parts, axis=0)

    base = len(NEAR)

    def halo_copy(n, index):
        col, d = HALO[index]
        block, e, _ = TARGETS[col]
        number = base + n * len(HALO) + index
        return pltpu.make_async_remote_copy(
            src_ref=vec.at[n, 2, block + 1],
            dst_ref=vec.at[n, 2 - d, col],
            send_sem=send_sem.at[number],
            recv_sem=recv_sem.at[number],
            device_id=(at_space(d), at_pair(e)),
            device_id_type=MESH,
        )

    def send(n, block):
        for index, (col, _) in enumerate(HALO):
            if TARGETS[col][0] == block:
                halo_copy(n, index).start()

    for a in range(2):
        for step in range(3):
            for row in (2, 3, 4):
                weigh(a, row, step)

    lax.fori_loop(0, 4, widen_own, 0)

    def build_own(group, carry):
        a = group // (TILES // BUILD)
        part = pl.ds((group - a * (TILES // BUILD)) * BUILD, BUILD)
        totals = zeros(BUILD)
        for step in range(3):
            for c in range(2):
                totals = build(a, part, 2, step, c, totals, step == 1, True)
        store_acc(a, part, totals)
        return carry

    lax.fori_loop(0, 2 * (TILES // BUILD), build_own, 0)
    for index, d in enumerate(NEAR):
        attr_copy(index, d).wait_recv()
    for a in range(2):
        for step in range(3):
            for row in (0, 1):
                weigh(a, row, step)
    lax.fori_loop(0, 16, widen_rest, 0)

    def build_rest(a, carry):
        def one_group(group, inner):
            part = pl.ds(group * BUILD, BUILD)

            totals = load_acc(a, part)
            for row in OTHERS:
                for step in range(3):
                    for c in range(2):
                        masked = (row, step) in ((1, 0), (3, 2))
                        totals = build(a, part, row, step, c, totals, False, masked)
            store_acc(a, part, totals)
            return inner

        lax.fori_loop(0, TILES // BUILD, one_group, 0)
        value = summed(a, False)
        direct[a] = value
        vec[0, 2, a + 1] = value * alpha[a]
        for block in range(2):

            @pl.when(a == block)
            def _():
                send(0, block)

        return carry

    lax.fori_loop(0, 2, build_rest, 0)

    def take(n, row, col):
        tile = vec[n, row, col]
        for m in range(6):
            spread[row, col, m] = jnp.broadcast_to(tile[m : m + 1, :], (SUBS, LANES))
        high = tile.astype(jnp.bfloat16).astype(jnp.float32)
        rest = tile - high
        middle = rest.astype(jnp.bfloat16).astype(jnp.float32)
        low = rest - middle
        parts = jnp.concatenate([high, middle, low, jnp.zeros_like(low)], axis=0)
        lanes = pl.ds((col * 5 + place(row)) * LANES, LANES)
        pieces[:, lanes] = parts.astype(jnp.bfloat16)

    def ready(n, col):
        for index, (far, d) in enumerate(HALO):
            if far == col:
                halo_copy(n, index).wait_recv()
                take(n, 2 - d, col)

    def strips(a, steps, rows, fresh):
        first, last = (place(rows[0]), place(rows[-1]) + 1)
        if fresh:
            cubed[a] = jnp.zeros((2, 4 * SUBS, BLK), jnp.float32)

        def one_group(group, carry):
            part = pl.ds(group * APPLY, APPLY)
            c = group // 2
            product = None
            for step in steps:
                own = (a + step) * 5
                term = lax.dot_general(
                    pieces[:, (own + first) * LANES : (own + last) * LANES],
                    cubes[
                        a, group, :, (step * 5 + first) * LANES : (step * 5 + last) * LANES
                    ],
                    (((1,), (1,)), ((), ())),
                    preferred_element_type=jnp.float32,
                )
                product = term if product is None else product + term
            totals = zeros(APPLY) if fresh else load_acc(a, part)
            for step in steps:
                for row in rows:
                    for k in range(2):
                        totals = apply(a, part, row, step, k, totals)
            store_acc(a, part, totals)
            cubed[a, c] = cubed[a, c] + product
            return carry

        lax.fori_loop(0, TILES // APPLY, one_group, 0)

    def finish(n, a):
        value = summed(a, True)
        field[n, a] = value
        vec[n + 1, 2, a + 1] = value * alpha[a]

        @pl.when(n + 1 < SWEEPS)
        def _():
            send(n + 1, a)

    def sweep(n, carry):
        take(n, 2, 1)
        take(n, 2, 2)
        strips(0, (1, 2), (2,), True)
        strips(1, (0, 1), (2,), True)
        ready(n, 1)
        strips(0, (1,), OTHERS, False)
        strips(1, (0,), OTHERS, False)
        ready(n, 2)
        strips(1, (1,), OTHERS, False)
        strips(0, (2,), OTHERS, False)
        ready(n, 0)
        strips(0, (0,), EVERY, False)
        finish(n, 0)
        ready(n, 3)
        strips(1, (2,), EVERY, False)
        finish(n, 1)
        return carry

    lax.fori_loop(0, SWEEPS, sweep, 0)

    lines = []
    for i, j in GRAM:
        product = field[i, 0] * (alpha[0] * field[j, 0]) + field[i, 1] * (alpha[1] * field[j, 1])
        lines.append(jnp.sum(product, axis=0, keepdims=True))
    lines.append(jnp.zeros((16 - len(GRAM), LANES), jnp.float32))
    total = jnp.concatenate(lines, axis=0)
    first = base + SWEEPS * len(HALO)
    pending = [attr_copy(index, d) for index, d in enumerate(NEAR)]
    for stage, (members, mine) in enumerate(stages):
        gram[stage, mine] = total
        copies = []
        for index, member in enumerate(members):
            copies.append(
                pltpu.make_async_remote_copy(
                    src_ref=gram.at[stage, mine],
                    dst_ref=gram.at[stage, mine],
                    send_sem=send_sem.at[first + index],
                    recv_sem=recv_sem.at[first + index],
                    device_id=member,
                    device_id_type=MESH,
                )
            )
            copies[-1].start()
        if stage == 0:

            def sent(n, carry):
                for index in range(len(HALO)):
                    halo_copy(n, index).wait_send()
                return carry

            lax.fori_loop(0, SWEEPS, sent, 0)
        for copy in pending:
            copy.wait_send()
        pending = copies
        for copy in copies:
            copy.wait_recv()
        first += len(members)
        total = gram[stage, 0]
        for index in range(1, len(members) + 1):
            total = total + gram[stage, index]

    sums = jnp.broadcast_to(jnp.sum(total, axis=1, keepdims=True), (16, LANES))
    entry = {}
    for index, (i, j) in enumerate(GRAM):
        entry[i, j] = entry[j, i] = sums[index : index + 1, :]

    def inner(left, right):
        value = None
        for i, u in enumerate(left):
            for j, v in enumerate(right):
                term = u * v * entry[i, j]
                value = term if value is None else value + term
        return value

    one = jnp.ones((1, LANES), jnp.float32)
    residual, direction = [one], [one]
    dipole = []
    rz_value = inner(residual, residual)
    for iteration in range(ITERS):
        size = iteration + 1
        image = [
            (direction[k] if k < size else 0.0) - (direction[k - 1] if k > 0 else 0.0)
            for k in range(size + 1)
        ]
        length = rz_value / inner(direction, image)
        dipole = [
            length * direction[k] + (dipole[k] if k < len(dipole) else 0.0) for k in range(size)
        ]
        residual = [
            (residual[k] if k < size else 0.0) - length * image[k] for k in range(size + 1)
        ]
        if iteration + 1 < ITERS:
            rz_next = inner(residual, residual)
            ratio = rz_next / rz_value
            direction = [
                residual[k] + (ratio * direction[k] if k < size else 0.0) for k in range(size + 1)
            ]
            rz_value = rz_next

    for a in range(2):
        moved = direct[a]
        for k in range(ITERS):
            moved = moved + dipole[k] * field[k, a]
        moved = moved * alpha[a]
        left = residual[0] * field[0, a]
        for k in range(1, ITERS + 1):
            left = left + residual[k] * field[k, a]
        for k in range(3):
            for c in range(2):
                lanes = slice(a * BLK + c * LANES, a * BLK + (c + 1) * LANES)
                dip_ref[k : k + 1, lanes] = moved[2 * k + c : 2 * k + c + 1, :]
                res_ref[k : k + 1, lanes] = left[2 * k + c : 2 * k + c + 1, :]
    for copy in pending:
        copy.wait_send()


def on_device(spaces, pairs, span_y, positions, polarizability, charges, groups, pair_list, tile_count):
    atoms = positions.shape[1]
    listed = pair_list.shape[1]
    copies = len(NEAR) + SWEEPS * len(HALO) + 2 * pairs + span_y + spaces // (2 * span_y) - 3
    share = jax.ShapeDtypeStruct((3, 2 * BLK), jnp.float32)
    vmem = pl.BlockSpec(memory_space=pltpu.VMEM)
    hbm = pl.BlockSpec(memory_space=pltpu.HBM)
    return pl.pallas_call(
        functools.partial(kernel, spaces, pairs, span_y),
        out_shape=(share, share),
        in_specs=[hbm] * 5 + [pl.BlockSpec(memory_space=pltpu.SMEM)],
        out_specs=(vmem, vmem),
        scratch_shapes=[
            pltpu.VMEM((3, atoms), jnp.float32),
            pltpu.VMEM((1, atoms), jnp.float32),
            pltpu.VMEM((1, atoms), jnp.float32),
            pltpu.VMEM((1, atoms), jnp.int32),
            pltpu.VMEM((2, listed), jnp.int32),
            pltpu.VMEM((32, LANES), jnp.float32),
            pltpu.VMEM((5, 4, 3, SUBS, LANES), jnp.float32),
            pltpu.VMEM((5, 4, 2, 6, SUBS, LANES), jnp.float32),
            pltpu.VMEM((2, 5, TILES, SUBS, LANES), jnp.float32),
            pltpu.VMEM((30, 2, SUBS, LANES), jnp.float32),
            pltpu.VMEM((60, 3, TILES, SUBS, LANES), jnp.float32),
            pltpu.VMEM((2, 4, BLK, 15 * LANES), jnp.bfloat16),
            pltpu.VMEM((2, 2, 4 * SUBS, BLK), jnp.float32),
            pltpu.VMEM((2, 3, TILES, SUBS, LANES), jnp.float32),
            pltpu.VMEM((2, 8, LANES), jnp.float32),
            pltpu.VMEM((2, 8, LANES), jnp.float32),
            pltpu.VMEM((SWEEPS + 1, 5, 4, SUBS, LANES), jnp.float32),
            pltpu.VMEM((5, 4, 6, SUBS, LANES), jnp.float32),
            pltpu.VMEM((4 * SUBS, 20 * LANES), jnp.bfloat16),
            pltpu.VMEM((SWEEPS, 2, 8, LANES), jnp.float32),
            pltpu.VMEM((3, 8, 16, LANES), jnp.float32),
            pltpu.SemaphoreType.DMA((5,)),
            pltpu.SemaphoreType.DMA((copies,)),
            pltpu.SemaphoreType.DMA((copies,)),
        ],
        compiler_params=pltpu.CompilerParams(
            collective_id=0, has_side_effects=True, vmem_limit_bytes=52 * 2**20
        ),
    )(
        *[
            pltpu.with_memory_space_constraint(value, pltpu.HBM)
            for value in (
                positions,
                polarizability[None],
                charges[None],
                groups[None],
                pair_list[0].T,
            )
        ],
        tile_count,
    )


def solution(mesh):
    spaces, pairs = mesh.shape["space"], mesh.shape["pair"]
    span_y = 8 if spaces >= 128 else 2
    return jax.shard_map(
        functools.partial(on_device, spaces, pairs, span_y),
        mesh=mesh,
        in_specs=(
            P(None, "space"),
            P("space"),
            P("space"),
            P("space"),
            P("space", None, None),
            P("space"),
        ),
        out_specs=(P(None, ("space", "pair")), P(None, ("space", "pair"))),
        check_vma=False,
    )
```

```python
import functools

import jax
import jax.numpy as jnp
from jax import lax
from jax.experimental import pallas as pl
from jax.experimental.pallas import tpu as pltpu
from jax.sharding import PartitionSpec as P

BLK = 256
BPD = 8
ITERS = 3
LANES = 128
SUBS = 8
TILES = BLK // SUBS
BUILD = 4
APPLY = 8
PERIOD = BPD * 8 * 2.15
THOLE = 0.39
ROOT_THREE = 3.0**0.5
SWEEPS = ITERS + 1
MESH = pl.DeviceIdType.MESH

NEAR = [-2, -1, 1, 2]
REACH = [-2, 2, -1, 1, 0]
TARGETS = {1: (0, 0, NEAR), 3: (0, -1, REACH), 2: (1, 0, NEAR), 0: (1, 1, REACH)}
HALO = [(column, d) for column in (1, 3, 2, 0) for d in TARGETS[column][2]]
X, Y, Z, GROUP, ROOT, CHARGE = range(6)
OTHERS = (0, 1, 3, 4)
EVERY = OTHERS + (2,)
GRAM = [(i, j) for i in range(ITERS) for j in range(i, ITERS + 1)]


def kernel(
    spaces,
    pairs,
    span_y,
    positions_ref,
    polar_ref,
    charges_ref,
    groups_ref,
    list_ref,
    count_ref,
    dip_ref,
    res_ref,
    positions,
    polar,
    charges,
    groups,
    listing,
    flags,
    window,
    wide,
    column,
    weight,
    coef,
    cubes,
    cubed,
    acc,
    alpha,
    direct,
    vec,
    spread,
    pieces,
    field,
    gram,
    load_sem,
    send_sem,
    recv_sem,
):
    loads = [
        pltpu.make_async_copy(source, target, load_sem.at[index])
        for index, (source, target) in enumerate(
            (
                (positions_ref, positions),
                (polar_ref, polar),
                (charges_ref, charges),
                (groups_ref, groups),
                (list_ref, listing),
            )
        )
    ]
    for load in loads:
        load.start()

    sp = lax.axis_index("space")
    pr = lax.axis_index("pair")
    core = lax.rem(sp, 2)
    y = lax.rem(sp // 2, span_y)
    z = sp // (2 * span_y)
    span_z = spaces // (2 * span_y)

    def at_space(d):
        return lax.rem(sp + (d + spaces), spaces)

    def at_pair(e):
        return lax.rem(pr + (e + pairs), pairs)

    def at_core(c):
        return sp - core + lax.rem(core + c, 2)

    stages = [
        (
            [(at_core(c), at_pair(k)) for k in range(pairs) for c in range(2) if (k, c) != (0, 0)],
            pr * 2 + core,
        ),
        (
            [(sp + (lax.rem(y + k, span_y) - y) * 2, pr) for k in range(1, span_y)],
            y,
        ),
        (
            [(sp + (lax.rem(z + k, span_z) - z) * 2 * span_y, pr) for k in range(1, span_z)],
            z,
        ),
    ]

    barrier = pltpu.get_barrier_semaphore()
    partners = [(at_space(d), at_pair(e)) for d in REACH for e in (-1, 0, 1) if (d, e) != (0, 0)]
    for members, _ in stages:
        partners = partners + members
    for partner in partners:
        pl.semaphore_signal(barrier, inc=1, device_id=partner, device_id_type=MESH)

    for load in loads:
        load.wait()

    slot, partner = listing[0:1, :], listing[1:2, :]
    row_step = (partner >> 3) - sp
    col_step = (((partner & 7) - slot + (BPD + 1)) & 7) - 1
    kind = jnp.where(row_step == 0, col_step, row_step * 3 + col_step)
    entry = lax.broadcasted_iota(jnp.int32, slot.shape, 1)
    key = jnp.where(entry < count_ref[0], kind * BPD + slot, -1)
    wanted = lax.broadcasted_iota(jnp.int32, (32, slot.shape[1]), 0)
    wanted = (wanted >> 2) * BPD + ((2 * pr + (BPD - 1) + (wanted & 3)) & 7)
    found = jnp.max((key == wanted).astype(jnp.float32), axis=1, keepdims=True)
    flags[...] = jnp.broadcast_to(found, (32, LANES))

    low = jnp.where(pr == 0, -PERIOD, 0.0).astype(jnp.float32)
    high = jnp.where(pr == pairs - 1, PERIOD, 0.0).astype(jnp.float32)
    for k in range(4):
        block = lax.rem(2 * pr + (k - 1 + BPD), BPD)
        for c in range(2):
            lanes = pl.ds(pl.multiple_of(block * BLK + c * LANES, LANES), LANES)
            shift = {0: low, 3: high}.get(k, 0.0)
            lines = {
                X: positions[0:1, lanes] + shift,
                Y: positions[1:2, lanes],
                Z: positions[2:3, lanes],
                GROUP: groups[0:1, lanes].astype(jnp.float32),
                ROOT: lax.rsqrt(polar[0:1, lanes]),
                CHARGE: charges[0:1, lanes],
            }
            for line, value in lines.items():
                window[2, k, c, line : line + 1, :] = value
            window[2, k, c, 6:8, :] = jnp.zeros((2, LANES), jnp.float32)
            if k in (1, 2):
                for m in range(3):
                    alpha[k - 1, 2 * m + c : 2 * m + c + 1, :] = polar[0:1, lanes]
        for m in range(8):
            window[2, k, 2, m : m + 1, :] = flags[4 * m + k : 4 * m + k + 1, :]

    def place(row):
        return EVERY.index(row)

    def widen(row, col):
        for c in range(2):
            for k in range(6):
                line = window[row, col, c, k : k + 1, :]
                wide[row, col, c, k] = jnp.broadcast_to(line, (SUBS, LANES))

    def widen_own(col, carry):
        widen(2, col)
        return carry

    pl.semaphore_wait(barrier, len(partners))

    def attr_copy(index, d):
        return pltpu.make_async_remote_copy(
            src_ref=window.at[2],
            dst_ref=window.at[2 - d],
            send_sem=send_sem.at[index],
            recv_sem=recv_sem.at[index],
            device_id=(at_space(d), pr),
            device_id_type=MESH,
        )

    for index in (1, 2, 0, 3):
        attr_copy(index, NEAR[index]).start()

    for a in range(2):
        for c in range(2):
            turned = window[2, a + 1, c].T
            for k in (X, Y, Z, GROUP, ROOT):
                values = jnp.broadcast_to(turned[:, k : k + 1], (LANES, LANES))
                if k == ROOT:
                    values = values * -THOLE
                half = LANES // SUBS
                column[a, k, c * half : (c + 1) * half] = values.reshape(half, SUBS, LANES)
        alpha[a, 6:8, :] = jnp.zeros((2, LANES), jnp.float32)

    def weigh(a, row, step):
        slot = a * 15 + row * 3 + step
        dx = step - 1
        if row == 2:
            entry, col = (abs(dx), a + step if dx < 0 else a + 1)
        elif row > 2:
            entry, col = ((2, 5)[row - 3] + dx + 1, a + 1)
        else:
            entry, col = ((5, 2)[row] - dx + 1, a + step)
        line = window[min(row, 2), col, 2, entry : entry + 1, :]
        weight[slot, 0] = jnp.broadcast_to(line, (SUBS, LANES))
        weight[slot, 1] = jnp.broadcast_to(line * ROOT_THREE, (SUBS, LANES))

    def build(a, part, row, step, c, totals, itself, masked):
        def far(line):
            return wide[row, a + step, c, line]

        rx = column[a, X, part] - far(X)
        ry = column[a, Y, part] - far(Y)
        rz = column[a, Z, part] - far(Z)
        squared = rx * rx + ry * ry + rz * rz
        if itself:
            squared = jnp.maximum(squared, 1.0)
        inverse = lax.rsqrt(squared)
        inverse_sq = inverse * inverse
        damping = (squared * (squared * inverse)) * (column[a, ROOT, part] * far(ROOT))
        decayed = jnp.exp(damping)
        third = 1.0 - decayed
        fifth = (third + damping * decayed) * inverse
        tile = a * 15 + row * 3 + step
        three = (third * (inverse_sq * inverse)) * weight[tile, 0]
        root = (fifth * lax.rsqrt(fifth)) * (inverse_sq * weight[tile, 1])
        index = tile * 2 + c
        coef[index, 0, part] = rx * root
        coef[index, 1, part] = ry * root
        coef[index, 2, part] = rz * root
        if itself:
            shape = (BUILD, SUBS, LANES)
            own = lax.broadcasted_iota(jnp.int32, shape, 0) * SUBS + part.start * SUBS
            own = own + lax.broadcasted_iota(jnp.int32, shape, 1)
            other = lax.broadcasted_iota(jnp.int32, shape, 2) + c * LANES
            three = jnp.where(own == other, 0.0, three)
        flat = three.reshape(BUILD * SUBS, LANES)
        high = flat.astype(jnp.bfloat16)
        low = (flat - high.astype(jnp.float32)).astype(jnp.bfloat16)
        first = pl.multiple_of(part.start * SUBS, BUILD * SUBS)
        rows = pl.ds(first, BUILD * SUBS)
        lanes = pl.ds(pl.multiple_of((step * 5 + place(row)) * LANES, LANES), LANES)
        cubes[a, 2 * c, rows, lanes] = high
        cubes[a, 2 * c + 1, rows, lanes] = low
        charged = three * far(CHARGE)
        if masked:
            charged = jnp.where(column[a, GROUP, part] != far(GROUP), charged, 0.0)
        ex, ey, ez = totals
        return (ex + charged * rx, ey + charged * ry, ez + charged * rz)

    def apply(a, part, row, step, c, totals):
        index = (a * 15 + row * 3 + step) * 2 + c
        sx, sy, sz = (coef[index, k, part] for k in range(3))
        vx, vy, vz = (spread[row, a + step, 2 * k + c] for k in range(3))
        along = sx * vx + sy * vy + sz * vz
        ex, ey, ez = totals
        return (ex + along * sx, ey + along * sy, ez + along * sz)

    def zeros(size):
        return tuple(jnp.zeros((size, SUBS, LANES), jnp.float32) for _ in range(3))

    def load_acc(a, part):
        return tuple(acc[a, k, part] for k in range(3))

    def store_acc(a, part, totals):
        for k in range(3):
            acc[a, k, part] = totals[k]

    def summed(a, with_cubes):
        if with_cubes:
            less = [
                cubed[a, c, 0:8] + cubed[a, c, 8:16] + cubed[a, c, 16:24] for c in range(2)
            ]
        parts = []
        for k in range(3):
            for c in range(2):
                half = LANES // SUBS
                turned = acc[a, k, c * half : (c + 1) * half].reshape(LANES, LANES).T
                part = jnp.sum(turned, axis=0, keepdims=True)
                if with_cubes:
                    lanes = slice(c * LANES, (c + 1) * LANES)
                    part = part - (
                        less[0][2 * k : 2 * k + 1, lanes] + less[1][2 * k + 1 : 2 * k + 2, lanes]
                    )
                parts.append(part)
        parts.append(jnp.zeros((2, LANES), jnp.float32))
        return jnp.concatenate(parts, axis=0)

    base = len(NEAR)

    def halo_copy(n, index):
        col, d = HALO[index]
        block, e, _ = TARGETS[col]
        number = base + n * len(HALO) + index
        return pltpu.make_async_remote_copy(
            src_ref=vec.at[n, 2, block + 1],
            dst_ref=vec.at[n, 2 - d, col],
            send_sem=send_sem.at[number],
            recv_sem=recv_sem.at[number],
            device_id=(at_space(d), at_pair(e)),
            device_id_type=MESH,
        )

    def send(n, block):
        for index, (col, _) in enumerate(HALO):
            if TARGETS[col][0] == block:
                halo_copy(n, index).start()

    for a in range(2):
        for step in range(3):
            for row in (2, 3, 4):
                weigh(a, row, step)

    lax.fori_loop(0, 4, widen_own, 0)

    def build_own(group, carry):
        a = group // (TILES // BUILD)
        part = pl.ds((group - a * (TILES // BUILD)) * BUILD, BUILD)
        totals = zeros(BUILD)
        for step in range(3):
            for c in range(2):
                totals = build(a, part, 2, step, c, totals, step == 1, True)
        store_acc(a, part, totals)
        return carry

    lax.fori_loop(0, 2 * (TILES // BUILD), build_own, 0)

    def build_rows(a, rows):
        def one_group(group, carry):
            part = pl.ds(group * BUILD, BUILD)
            totals = load_acc(a, part)
            for row in rows:
                for step in range(3):
                    for c in range(2):
                        masked = (row, step) in ((1, 0), (3, 2))
                        totals = build(a, part, row, step, c, totals, False, masked)
            store_acc(a, part, totals)
            return carry

        lax.fori_loop(0, TILES // BUILD, one_group, 0)

    def arrived(rows):
        for row in rows:
            attr_copy(NEAR.index(2 - row), 2 - row).wait_recv()
        for a in range(2):
            for step in range(3):
                weigh(a, min(rows), step)

        def widen_rows(col, carry):
            for row in rows:
                widen(row, col)
            return carry

        lax.fori_loop(0, 4, widen_rows, 0)

    def build_next(a, carry):
        build_rows(a, (1, 3))
        return carry

    def build_last(a, carry):
        build_rows(a, (0, 4))
        value = summed(a, False)
        direct[a] = value
        vec[0, 2, a + 1] = value * alpha[a]
        for block in range(2):

            @pl.when(a == block)
            def _():
                send(0, block)

        return carry

    arrived((1, 3))
    lax.fori_loop(0, 2, build_next, 0)
    arrived((0, 4))
    lax.fori_loop(0, 2, build_last, 0)

    def take(n, row, col):
        tile = vec[n, row, col]
        for m in range(6):
            spread[row, col, m] = jnp.broadcast_to(tile[m : m + 1, :], (SUBS, LANES))
        high = tile.astype(jnp.bfloat16).astype(jnp.float32)
        rest = tile - high
        middle = rest.astype(jnp.bfloat16).astype(jnp.float32)
        low = rest - middle
        parts = jnp.concatenate([high, middle, low, jnp.zeros_like(low)], axis=0)
        lanes = pl.ds((col * 5 + place(row)) * LANES, LANES)
        pieces[:, lanes] = parts.astype(jnp.bfloat16)

    def ready(n, col):
        for index, (far, d) in enumerate(HALO):
            if far == col:
                halo_copy(n, index).wait_recv()
                take(n, 2 - d, col)

    def strips(a, steps, rows, fresh):
        first, last = (place(rows[0]), place(rows[-1]) + 1)
        if fresh:
            cubed[a] = jnp.zeros((2, 4 * SUBS, BLK), jnp.float32)

        def one_group(group, carry):
            part = pl.ds(group * APPLY, APPLY)
            c = group // 2
            product = None
            for step in steps:
                own = (a + step) * 5
                term = lax.dot_general(
                    pieces[:, (own + first) * LANES : (own + last) * LANES],
                    cubes[
                        a, group, :, (step * 5 + first) * LANES : (step * 5 + last) * LANES
                    ],
                    (((1,), (1,)), ((), ())),
                    preferred_element_type=jnp.float32,
                )
                product = term if product is None else product + term
            totals = zeros(APPLY) if fresh else load_acc(a, part)
            for step in steps:
                for row in rows:
                    for k in range(2):
                        totals = apply(a, part, row, step, k, totals)
            store_acc(a, part, totals)
            cubed[a, c] = cubed[a, c] + product
            return carry

        lax.fori_loop(0, TILES // APPLY, one_group, 0)

    def finish(n, a):
        value = summed(a, True)
        field[n, a] = value
        vec[n + 1, 2, a + 1] = value * alpha[a]

        @pl.when(n + 1 < SWEEPS)
        def _():
            send(n + 1, a)

    def sweep(n, carry):
        take(n, 2, 1)
        take(n, 2, 2)
        strips(0, (1, 2), (2,), True)
        strips(1, (0, 1), (2,), True)
        ready(n, 1)
        strips(0, (1,), OTHERS, False)
        strips(1, (0,), OTHERS, False)
        ready(n, 2)
        strips(1, (1,), OTHERS, False)
        strips(0, (2,), OTHERS, False)
        ready(n, 0)
        strips(0, (0,), EVERY, False)
        finish(n, 0)
        ready(n, 3)
        strips(1, (2,), EVERY, False)
        finish(n, 1)
        return carry

    lax.fori_loop(0, SWEEPS, sweep, 0)

    lines = []
    for i, j in GRAM:
        product = field[i, 0] * (alpha[0] * field[j, 0]) + field[i, 1] * (alpha[1] * field[j, 1])
        lines.append(jnp.sum(product, axis=0, keepdims=True))
    lines.append(jnp.zeros((16 - len(GRAM), LANES), jnp.float32))
    total = jnp.concatenate(lines, axis=0)
    first = base + SWEEPS * len(HALO)
    pending = [attr_copy(index, d) for index, d in enumerate(NEAR)]
    for stage, (members, mine) in enumerate(stages):
        gram[stage, mine] = total
        copies = []
        for index, member in enumerate(members):
            copies.append(
                pltpu.make_async_remote_copy(
                    src_ref=gram.at[stage, mine],
                    dst_ref=gram.at[stage, mine],
                    send_sem=send_sem.at[first + index],
                    recv_sem=recv_sem.at[first + index],
                    device_id=member,
                    device_id_type=MESH,
                )
            )
            copies[-1].start()
        if stage == 0:

            def sent(n, carry):
                for index in range(len(HALO)):
                    halo_copy(n, index).wait_send()
                return carry

            lax.fori_loop(0, SWEEPS, sent, 0)
        for copy in pending:
            copy.wait_send()
        pending = copies
        for copy in copies:
            copy.wait_recv()
        first += len(members)
        total = gram[stage, 0]
        for index in range(1, len(members) + 1):
            total = total + gram[stage, index]

    sums = jnp.broadcast_to(jnp.sum(total, axis=1, keepdims=True), (16, LANES))
    entry = {}
    for index, (i, j) in enumerate(GRAM):
        entry[i, j] = entry[j, i] = sums[index : index + 1, :]

    def inner(left, right):
        value = None
        for i, u in enumerate(left):
            for j, v in enumerate(right):
                term = u * v * entry[i, j]
                value = term if value is None else value + term
        return value

    one = jnp.ones((1, LANES), jnp.float32)
    residual, direction = [one], [one]
    dipole = []
    rz_value = inner(residual, residual)
    for iteration in range(ITERS):
        size = iteration + 1
        image = [
            (direction[k] if k < size else 0.0) - (direction[k - 1] if k > 0 else 0.0)
            for k in range(size + 1)
        ]
        length = rz_value / inner(direction, image)
        dipole = [
            length * direction[k] + (dipole[k] if k < len(dipole) else 0.0) for k in range(size)
        ]
        residual = [
            (residual[k] if k < size else 0.0) - length * image[k] for k in range(size + 1)
        ]
        if iteration + 1 < ITERS:
            rz_next = inner(residual, residual)
            ratio = rz_next / rz_value
            direction = [
                residual[k] + (ratio * direction[k] if k < size else 0.0) for k in range(size + 1)
            ]
            rz_value = rz_next

    for a in range(2):
        moved = direct[a]
        for k in range(ITERS):
            moved = moved + dipole[k] * field[k, a]
        moved = moved * alpha[a]
        left = residual[0] * field[0, a]
        for k in range(1, ITERS + 1):
            left = left + residual[k] * field[k, a]
        for k in range(3):
            for c in range(2):
                lanes = slice(a * BLK + c * LANES, a * BLK + (c + 1) * LANES)
                dip_ref[k : k + 1, lanes] = moved[2 * k + c : 2 * k + c + 1, :]
                res_ref[k : k + 1, lanes] = left[2 * k + c : 2 * k + c + 1, :]
    for copy in pending:
        copy.wait_send()


def on_device(spaces, pairs, span_y, positions, polarizability, charges, groups, pair_list, tile_count):
    atoms = positions.shape[1]
    listed = pair_list.shape[1]
    copies = len(NEAR) + SWEEPS * len(HALO) + 2 * pairs + span_y + spaces // (2 * span_y) - 3
    share = jax.ShapeDtypeStruct((3, 2 * BLK), jnp.float32)
    vmem = pl.BlockSpec(memory_space=pltpu.VMEM)
    hbm = pl.BlockSpec(memory_space=pltpu.HBM)
    return pl.pallas_call(
        functools.partial(kernel, spaces, pairs, span_y),
        out_shape=(share, share),
        in_specs=[hbm] * 5 + [pl.BlockSpec(memory_space=pltpu.SMEM)],
        out_specs=(vmem, vmem),
        scratch_shapes=[
            pltpu.VMEM((3, atoms), jnp.float32),
            pltpu.VMEM((1, atoms), jnp.float32),
            pltpu.VMEM((1, atoms), jnp.float32),
            pltpu.VMEM((1, atoms), jnp.int32),
            pltpu.VMEM((2, listed), jnp.int32),
            pltpu.VMEM((32, LANES), jnp.float32),
            pltpu.VMEM((5, 4, 3, SUBS, LANES), jnp.float32),
            pltpu.VMEM((5, 4, 2, 6, SUBS, LANES), jnp.float32),
            pltpu.VMEM((2, 5, TILES, SUBS, LANES), jnp.float32),
            pltpu.VMEM((30, 2, SUBS, LANES), jnp.float32),
            pltpu.VMEM((60, 3, TILES, SUBS, LANES), jnp.float32),
            pltpu.VMEM((2, 4, BLK, 15 * LANES), jnp.bfloat16),
            pltpu.VMEM((2, 2, 4 * SUBS, BLK), jnp.float32),
            pltpu.VMEM((2, 3, TILES, SUBS, LANES), jnp.float32),
            pltpu.VMEM((2, 8, LANES), jnp.float32),
            pltpu.VMEM((2, 8, LANES), jnp.float32),
            pltpu.VMEM((SWEEPS + 1, 5, 4, SUBS, LANES), jnp.float32),
            pltpu.VMEM((5, 4, 6, SUBS, LANES), jnp.float32),
            pltpu.VMEM((4 * SUBS, 20 * LANES), jnp.bfloat16),
            pltpu.VMEM((SWEEPS, 2, 8, LANES), jnp.float32),
            pltpu.VMEM((3, 8, 16, LANES), jnp.float32),
            pltpu.SemaphoreType.DMA((5,)),
            pltpu.SemaphoreType.DMA((copies,)),
            pltpu.SemaphoreType.DMA((copies,)),
        ],
        compiler_params=pltpu.CompilerParams(
            collective_id=0, has_side_effects=True, vmem_limit_bytes=52 * 2**20
        ),
    )(
        *[
            pltpu.with_memory_space_constraint(value, pltpu.HBM)
            for value in (
                positions,
                polarizability[None],
                charges[None],
                groups[None],
                pair_list[0].T,
            )
        ],
        tile_count,
    )


def solution(mesh):
    spaces, pairs = mesh.shape["space"], mesh.shape["pair"]
    span_y = 8 if spaces >= 128 else 2
    return jax.shard_map(
        functools.partial(on_device, spaces, pairs, span_y),
        mesh=mesh,
        in_specs=(
            P(None, "space"),
            P("space"),
            P("space"),
            P("space"),
            P("space", None, None),
            P("space"),
        ),
        out_specs=(P(None, ("space", "pair")), P(None, ("space", "pair"))),
        check_vma=False,
    )
```
